32 devices in a mesh: dp: 16 (over z, x, core), ctx: 2 (over y).
Axes of the slice: x: 2, y: 2, z: 4, core: 2. Of those that a mesh axis runs over, the one named last changes fastest.
Arguments:
- queries: bfloat16 [16384, 1024], P(('dp', 'ctx')), may hold values from -6 to 6
- keys_values: bfloat16 [16384, 1, 2, 128], P(('dp', 'ctx')), may hold values from -6 to 6
- routing: int32 [16384, 2], P(('dp', 'ctx')), may hold values from 0 to 511, as said below
- documents: int32 [16384], P(('dp', 'ctx')), may hold values from 0 to 16383, as said below
Outputs:
- attended: bfloat16 [16384, 1024], P(('dp', 'ctx'))
The draws below stay inside these ranges and needn't reach their ends.
Inputs may be any that keep to these rules, and one draw needn't show every extreme that they name: routing[r, 0] is the packed sequence and routing[r, 1] the position inside the 512-token block (the block at the owner's index along ctx) to which owner row r goes; every position is filled exactly once. Each aligned block of 64 rows of one owner goes, in order, to 64 consecutive positions of one destination, and different blocks of one owner go to different destinations. `documents`: A token's document id is 1024 times its packed sequence plus the position in that sequence at which its document begins; in every draw some sequence other than the last is one whole document, and every other sequence ends with a one-token document.
All inputs are finite; a program needn't handle non-finite values.
Results may differ from the reference program's by a relative error of at most 0.0045.
Values may be sent and summed in bfloat16 or wider, within the bound.
No kernel may reach another device: no remote copies, remote signals or barrier semaphores. Data moves between devices by JAX's collectives and lax.ppermute only.
A program may use at most 64 MiB of HBM per device.

```python
import math
import jax
import jax.numpy as jnp
from jax import lax

H = 8
KVH = 1
HD = 128
TOK_DEV = 512
QPG = 8
CAP = 64
SEQ_LEN = 1024
TOKENS = 16384
N_DP = 16
N_CTX = 2


def layout(key):
    blocks = TOK_DEV // CAP
    column_keys = jax.random.split(jax.random.fold_in(key, 101), N_CTX)
    shifts = jax.vmap(lambda inner: jax.random.permutation(inner, N_DP))(column_keys).astype(jnp.int32)
    owner_rows = jnp.arange(TOKENS, dtype=jnp.int32)
    device = owner_rows // TOK_DEV
    owner = device // N_CTX
    column = device % N_CTX
    owner_slot = owner_rows % TOK_DEV
    owner_block = owner_slot // CAP
    within = owner_slot % CAP
    block_index = (owner_block - owner) % blocks
    target = (owner - shifts[column, block_index]) % N_DP
    position = block_index * CAP + within
    packed = target * SEQ_LEN + column * TOK_DEV + position
    return (target, position, packed)


def doc_layout(key):
    first_key, second_key, third_key = jax.random.split(jax.random.fold_in(key, 202), 3)
    reach = jax.random.randint(first_key, (N_DP, 1), 8, SEQ_LEN + 1)
    single = jax.random.randint(second_key, (), 0, N_DP - 1)
    spots = jnp.arange(SEQ_LEN, dtype=jnp.int32)
    sequence = jnp.arange(N_DP, dtype=jnp.int32)[:, None]
    begins = jax.random.randint(third_key, (N_DP, SEQ_LEN), 0, reach) == 0
    begins = begins | (spots[None, :] == SEQ_LEN - 1)
    begins = begins & (sequence != single)
    begins = begins | (spots[None, :] == 0)
    first = lax.cummax(jnp.where(begins, spots[None, :], 0), axis=1)
    return (sequence * SEQ_LEN + first).reshape(TOKENS)


def draw_routing(key, part):
    target, position, packed = layout(key)
    return jnp.stack([target, position], axis=1).astype(jnp.int32)


def draw_documents(key, part):
    target, position, packed = layout(key)
    doc_ids = doc_layout(key)
    return doc_ids[packed].astype(jnp.int32)


def draw_queries(key, part):
    target, position, packed = layout(key)
    key = jax.random.fold_in(key, 5)
    values = jax.random.truncated_normal(key, -6.0, 6.0, (TOKENS, KVH, QPG, HD), jnp.float32)
    return values.reshape(TOKENS, H * HD)[packed].astype(jnp.bfloat16)


def draw_keys_values(key, part):
    target, position, packed = layout(key)
    key = jax.random.fold_in(key, 7)
    key_part, value_part = jax.random.split(key)
    keys = jax.random.truncated_normal(key_part, -6.0, 6.0, (TOKENS, KVH, HD), jnp.float32)
    values = jax.random.truncated_normal(value_part, -6.0, 6.0, (TOKENS, KVH, HD), jnp.float32)
    stacked = jnp.stack([keys, values], axis=2)
    return stacked[packed].astype(jnp.bfloat16)


def setup_inputs(seed: int = 0) -> dict:
    splits = jax.random.split(jax.random.key(seed), 5)
    queries = draw_queries(jax.random.fold_in(splits[4], 71), 0)
    keys_values = draw_keys_values(jax.random.fold_in(splits[4], 71), 0)
    routing = draw_routing(jax.random.fold_in(splits[4], 71), 0)
    documents = draw_documents(jax.random.fold_in(splits[4], 71), 0)
    return dict(queries=queries, keys_values=keys_values, routing=routing, documents=documents)


def one_group(operands):
    group_q, group_k, group_v, doc_ids = operands
    factor = 1.0 / math.sqrt(HD)
    positions = jnp.arange(SEQ_LEN, dtype=jnp.int32)
    keys_f = group_k.astype(jnp.float32)
    values_f = group_v.astype(jnp.float32)

    def one_block(index):
        start = (index * TOK_DEV).astype(jnp.int32)
        block_q = lax.dynamic_slice_in_dim(group_q, start, TOK_DEV, 0)
        block_doc = lax.dynamic_slice_in_dim(doc_ids, start, TOK_DEV, 0)
        block_pos = start + jnp.arange(TOK_DEV, dtype=jnp.int32)
        scores = jnp.einsum('tqd,kd->qtk', block_q.astype(jnp.float32), keys_f) * factor
        allowed = (block_pos[:, None] >= positions[None, :]) & (block_doc[:, None] == doc_ids[None, :])
        scores = jnp.where(allowed[None], scores, -1e+30)
        peaks = lax.optimization_barrier(jnp.max(scores, axis=-1, keepdims=True))
        weights = jnp.where(allowed[None], jnp.exp(scores - peaks), 0.0)
        totals = lax.optimization_barrier(jnp.sum(weights, axis=-1))
        rounded = weights.astype(jnp.bfloat16)
        mixed = jnp.einsum('qtk,kd->tqd', rounded.astype(jnp.float32), values_f)
        return (mixed / jnp.transpose(totals)[:, :, None]).astype(jnp.bfloat16)
    blocks = lax.map(one_block, jnp.arange(N_CTX, dtype=jnp.int32))
    return blocks.reshape(SEQ_LEN, QPG, HD)

def reference(queries, keys_values, routing, documents):
    owner_rows = jnp.arange(TOKENS, dtype=jnp.int32)
    columns = owner_rows // TOK_DEV % N_CTX
    packed = (routing[:, 0] * SEQ_LEN + columns * TOK_DEV + routing[:, 1]).astype(jnp.int32)
    packed_q = jnp.zeros_like(queries).at[packed].set(queries)
    packed_kv = jnp.zeros_like(keys_values).at[packed].set(keys_values)
    packed_doc = jnp.zeros((TOKENS,), jnp.int32).at[packed].set(documents)
    group_q = packed_q.reshape(N_DP, SEQ_LEN, KVH, QPG, HD).transpose(0, 2, 1, 3, 4).reshape(N_DP * KVH, SEQ_LEN, QPG, HD)
    group_kv = packed_kv.reshape(N_DP, SEQ_LEN, KVH, 2, HD).transpose(0, 2, 1, 3, 4).reshape(N_DP * KVH, SEQ_LEN, 2, HD)
    group_doc = jnp.repeat(packed_doc.reshape(N_DP, SEQ_LEN), KVH, axis=0)
    results = lax.map(one_group, (group_q, group_kv[:, :, 0], group_kv[:, :, 1], group_doc))
    return results.reshape(N_DP, KVH, SEQ_LEN, QPG, HD).transpose(0, 2, 1, 3, 4).reshape(TOKENS, H * HD)
```

```python
import functools
import math

import jax
import jax.numpy as jnp
from jax import lax
from jax.experimental import pallas as pl
from jax.experimental.pallas import tpu as pltpu
from jax.sharding import PartitionSpec as P

LANES = 128
LABEL_ROWS = 16
DIGIT = 64
TOGETHER = 4
APART = 16384.0
NEVER = -1e30
ANY = pl.BlockSpec(memory_space=pl.ANY)
VMEM = pl.BlockSpec(memory_space=pltpu.VMEM)
SMEM = pl.BlockSpec(memory_space=pltpu.SMEM)


def params(mib):
    return pltpu.CompilerParams(vmem_limit_bytes=mib * 1024 * 1024)


def hbm(*arrays):
    return [pltpu.with_memory_space_constraint(array, pltpu.HBM) for array in arrays]


def pack_kv(routing, documents, kv, owners, seq_len):
    rows = kv.shape[0] // 2
    cap = 2 * rows // owners
    blocks = rows // cap
    per_group = LANES // cap

    def kernel(routing_any, doc_any, kv_any, out_ref, routing_ref, doc_ref, kv_ref, label_ref, held_ref, in_sem, sem, label_sem):
        fetches = [
            pltpu.make_async_copy(source, target, in_sem.at[index])
            for index, (source, target) in enumerate(
                ((routing_any, routing_ref), (doc_any, doc_ref), (kv_any, kv_ref))
            )
        ]
        for fetch in fetches:
            fetch.start()
        fetches[0].wait()
        for slot in range(owners):
            held_ref[slot] = blocks
        for block in range(blocks):
            held_ref[routing_ref[0, block * cap]] = block
        fetches[1].wait()
        row_at = lax.broadcasted_iota(jnp.int32, (LABEL_ROWS, LANES), 0)
        label_ref[blocks] = jnp.full((LABEL_ROWS, LANES), 255.0, jnp.bfloat16)
        for block in range(blocks):
            group, part = divmod(block, per_group)
            begin = doc_ref[group : group + 1, :] - routing_ref[0, block * cap] * seq_len
            place = routing_ref[1, block * cap] // cap
            label = jnp.where(row_at == 0, begin // DIGIT, jnp.where(row_at == 1, begin % DIGIT, part))
            label = jnp.where(row_at == 2, place, label)
            label_ref[block] = label.astype(jnp.float32).astype(jnp.bfloat16)
        copies = [
            pltpu.make_async_copy(
                label_ref.at[held_ref[slot]], out_ref.at[slot, pl.ds(0, LABEL_ROWS)], label_sem.at[slot]
            )
            for slot in range(owners)
        ]
        for block in range(blocks):
            copies.append(
                pltpu.make_async_copy(
                    kv_ref.at[pl.ds(block * 2 * cap, 2 * cap)],
                    out_ref.at[routing_ref[0, block * cap], pl.ds(LABEL_ROWS, 2 * cap)],
                    sem.at[block],
                )
            )
        fetches[2].wait()
        for copy in copies:
            copy.start()
        for copy in copies:
            copy.wait()

    return pl.pallas_call(
        kernel,
        out_shape=pltpu.HBM((owners, LABEL_ROWS + 2 * cap, LANES), kv.dtype),
        in_specs=[ANY] * 3,
        out_specs=ANY,
        scratch_shapes=[
            pltpu.SMEM(routing.shape, jnp.int32),
            pltpu.VMEM(documents.shape, jnp.int32),
            pltpu.VMEM(kv.shape, kv.dtype),
            pltpu.VMEM((blocks + 1, LABEL_ROWS, LANES), jnp.bfloat16),
            pltpu.SMEM((owners,), jnp.int32),
            pltpu.SemaphoreType.DMA((3,)),
            pltpu.SemaphoreType.DMA((blocks,)),
            pltpu.SemaphoreType.DMA((owners,)),
        ],
        compiler_params=params(16),
        name="pack_kv",
    )(*hbm(routing, documents, kv))


def pack_q(routing, queries, earlier, owners):
    rows, width = queries.shape
    cap = 2 * rows // owners
    blocks = rows // cap
    half = owners // 2

    def kernel(routing_any, q_any, earlier_ref, near_ref, *rest):
        far_refs = rest[:half]
        routing_ref, q_ref, held_ref, in_sem, q_sem, sem = rest[half:]
        me = lax.axis_index("dp")
        fetch = pltpu.make_async_copy(routing_any, routing_ref, in_sem)
        fetch.start()
        fetch_q = pltpu.make_async_copy(q_any, q_ref, q_sem)
        fetch_q.start()
        fetch.wait()
        for slot in range(owners):
            held_ref[slot] = blocks
        for block in range(blocks):
            held_ref[routing_ref[0, block * cap]] = block
        copies = []
        for step in range(owners):
            slot = me ^ step
            block = held_ref[slot]
            q_rows = pl.ds(pl.multiple_of(jnp.minimum(block, blocks - 1) * cap, cap), cap)
            target = far_refs[step - half] if step >= half else near_ref.at[lax.rem(slot, half)]
            copies.append((block < blocks, pltpu.make_async_copy(q_ref.at[q_rows], target, sem.at[step])))
        fetch_q.wait()
        for held, copy in copies:
            pl.when(held)(copy.start)
        for held, copy in copies:
            pl.when(held)(copy.wait)

    return pl.pallas_call(
        kernel,
        out_shape=[
            pltpu.HBM((half, cap, width), queries.dtype),
            *[jax.ShapeDtypeStruct((cap, width), queries.dtype)] * half,
        ],
        in_specs=[ANY] * 3,
        out_specs=[ANY] * (1 + half),
        scratch_shapes=[
            pltpu.SMEM(routing.shape, jnp.int32),
            pltpu.VMEM(queries.shape, queries.dtype),
            pltpu.SMEM((owners,), jnp.int32),
            pltpu.SemaphoreType.DMA,
            pltpu.SemaphoreType.DMA,
            pltpu.SemaphoreType.DMA((owners,)),
        ],
        compiler_params=params(16),
        name="pack_q",
    )(*hbm(routing, queries, earlier))


def place_kv(source, parcels, begins, rows, cap):
    blocks = rows // cap

    def kernel(source_ref, in_ref, begin_ref, out_ref, sem):
        copies = [
            pltpu.make_async_copy(
                in_ref.at[source_ref[place], pl.ds(LABEL_ROWS, 2 * cap)],
                out_ref.at[pl.ds(place * 2 * cap, 2 * cap)],
                sem.at[place],
            )
            for place in range(blocks)
        ]
        copies.append(
            pltpu.make_async_copy(begin_ref, out_ref.at[pl.ds(2 * rows, begin_ref.shape[0])], sem.at[blocks])
        )
        for copy in copies:
            copy.start()
        for copy in copies:
            copy.wait()

    return pl.pallas_call(
        kernel,
        out_shape=jax.ShapeDtypeStruct((2 * rows + begins.shape[0], LANES), parcels.dtype),
        in_specs=[SMEM, ANY, ANY],
        out_specs=ANY,
        scratch_shapes=[pltpu.SemaphoreType.DMA((blocks + 1,))],
        compiler_params=params(16),
        name="place_kv",
    )(source, parcels, begins)


def attend(meta, first, near, far, own, past, out):
    rows = own[0].shape[0]
    cap, width = far[0].shape
    blocks = rows // cap
    heads = width // LANES
    half = rows // 2
    count = past[0].shape[0]
    slots = 0 if near is None else near.shape[0]
    parcels = slots + len(far)
    factor = math.log2(math.e) / math.sqrt(LANES)
    arrays = ([] if near is None else [near]) + far

    def kernel(meta_ref, qd_ref, ok_ref, od_ref, ov_ref, pk_ref, pd_ref, pv_ref, *rest):
        array_refs = rest[: len(arrays)]
        out_any, stage_ref, result_ref, sem = rest[-4:]

        def keys(k_ref, d_ref):
            return jnp.concatenate([k_ref, d_ref], axis=1)

        def values(v):
            return jnp.concatenate([v, jnp.ones(v.shape, v.dtype)], axis=1)

        def scores(tile_q, tile_k):
            return lax.dot_general(tile_q, tile_k, (((1,), (1,)), ((), ())), preferred_element_type=jnp.float32)

        def top(raw):
            return jnp.max(raw, axis=-1, keepdims=True)

        def mix(raw, peak, tile_v):
            weights = jnp.exp2((raw - peak) * factor).astype(jnp.bfloat16)
            return jnp.dot(weights, tile_v, preferred_element_type=jnp.float32)

        def place_of(index):
            return meta_ref[1 + first + index]

        def result_copy(index):
            at = pl.multiple_of(jnp.minimum(place_of(index), blocks - 1) * cap, cap)
            return pltpu.make_async_copy(result_ref.at[index], out_any.at[pl.ds(at, cap)], sem.at[index])

        def one_block(index, place, lower, with_past):
            block_q = stage_ref[index]
            same = qd_ref[pl.ds(pl.multiple_of(place * cap, cap), cap), :]
            same = jnp.concatenate([same] * TOGETHER, axis=0)
            row_at = lax.broadcasted_iota(jnp.int32, (cap, half), 0) + (place * cap - lower * half)
            seen = lax.broadcasted_iota(jnp.int32, (cap, half), 1) <= row_at
            last = pl.ds(lower * half, half)

            def causal(raw):
                return jnp.where(seen[None], raw.reshape(TOGETHER, cap, half), NEVER).reshape(TOGETHER * cap, half)

            tile_qs = []
            for begin in range(0, heads, TOGETHER):
                tiles = [block_q[:, head * LANES : (head + 1) * LANES] for head in range(begin, begin + TOGETHER)]
                tile_qs.append(jnp.concatenate([jnp.concatenate(tiles, axis=0), same], axis=1))
            raws = [[causal(scores(tile_q, keys(ok_ref[last], od_ref[last])))] for tile_q in tile_qs]
            tile_vs = [ov_ref[last]]
            if lower:
                for several, tile_q in zip(raws, tile_qs):
                    several.append(scores(tile_q, keys(ok_ref[:half], od_ref[:half])))
                tile_vs.append(ov_ref[:half])
            if with_past:
                for several, tile_q in zip(raws, tile_qs):
                    several.append(scores(tile_q, keys(pk_ref[0], pd_ref[0])))
                tile_vs.append(pv_ref[0])
            peaks = [functools.reduce(jnp.maximum, [top(raw) for raw in several]) for several in raws]
            mixes = [
                sum(mix(raw, peak, values(tile_v)) for raw, tile_v in zip(several, tile_vs))
                for several, peak in zip(raws, peaks)
            ]
            if count > 1:

                def step(earlier, state):
                    result = []
                    for (peak, mixed), tile_q in zip(state, tile_qs):
                        raw = scores(tile_q, keys(pk_ref[earlier], pd_ref[earlier]))
                        higher = jnp.maximum(peak, top(raw))
                        decay = jnp.exp2((peak - higher) * factor)
                        result.append((higher, mixed * decay + mix(raw, higher, values(pv_ref[earlier]))))
                    return result

                mixes = [mixed for _, mixed in lax.fori_loop(0, meta_ref[0], step, list(zip(peaks, mixes)))]
            for at, mixed in enumerate(mixes):
                result = (mixed[:, :LANES] / mixed[:, LANES:]).astype(jnp.bfloat16)
                for head in range(TOGETHER):
                    column = (at * TOGETHER + head) * LANES
                    result_ref[index, :, column : column + LANES] = result[head * cap : (head + 1) * cap]

        def body(index, carry):
            place = place_of(index)
            for lower in (0, 1):
                here = (place < blocks) & (place >= blocks // 2) if lower else place < blocks // 2
                if count > 1:
                    pl.when(here)(functools.partial(one_block, index, place, lower, False))
                else:
                    for column in (0, 1):
                        pl.when(here & (meta_ref[0] == column))(
                            functools.partial(one_block, index, place, lower, column == 1)
                        )
            pl.when(place < blocks)(result_copy(index).start)
            return carry

        for index in range(parcels):

            @pl.when(place_of(index) < blocks)
            def _():
                stage_ref[index] = array_refs[0][index] if index < slots else array_refs[index - slots + (slots > 0)][...]

        lax.fori_loop(0, parcels, body, 0)
        for index in range(parcels):
            pl.when(place_of(index) < blocks)(result_copy(index).wait)

    operands = [meta, *own, *past, *arrays]
    specs = [SMEM] + [VMEM] * (len(operands) - 1)
    aliases = {}
    if out is not None:
        aliases = {len(operands): 0}
        operands.append(out)
        specs.append(ANY)
    area = max(1, parcels // 2) * heads * cap * (count + 1) * rows
    return pl.pallas_call(
        kernel,
        out_shape=jax.ShapeDtypeStruct((rows, width), jnp.bfloat16),
        in_specs=specs,
        out_specs=ANY,
        input_output_aliases=aliases,
        scratch_shapes=[
            pltpu.VMEM((parcels, cap, width), jnp.bfloat16),
            pltpu.VMEM((parcels, cap, width), jnp.bfloat16),
            pltpu.SemaphoreType.DMA((parcels,)),
        ],
        compiler_params=params(28),
        cost_estimate=pl.CostEstimate(
            flops=8 * area * LANES, bytes_accessed=4 * parcels * cap * width, transcendentals=area
        ),
        name="attend",
    )(*operands)


def digits(begin):
    lane = jnp.arange(LANES, dtype=jnp.int32)
    digit = jnp.where(lane < DIGIT, begin[..., None] // DIGIT, begin[..., None] % DIGIT)
    hit = digit == lane % DIGIT
    return jnp.where(hit, 1.0, 0.0).astype(jnp.bfloat16), jnp.where(hit, 0.0, -APART).astype(jnp.bfloat16)


def local(queries, keys_values, routing, documents):
    rows, width = queries.shape
    owners = lax.axis_size("dp")
    columns = lax.axis_size("ctx")
    kv_heads, pair, head_dim = keys_values.shape[1:]
    assert kv_heads == 1 and pair == 2 and head_dim == LANES
    cap = 2 * rows // owners
    blocks = rows // cap
    seq_len = rows * columns
    assert seq_len <= DIGIT * DIGIT
    half = owners // 2
    assert owners & (owners - 1) == 0
    column = lax.axis_index("ctx")
    me = lax.axis_index("dp")

    routing = routing.T
    send_kv = pack_kv(routing, documents.reshape(-1, LANES), keys_values.reshape(2 * rows, LANES), owners, seq_len)
    parcels = lax.all_to_all(send_kv, "dp", split_axis=0, concat_axis=0, tiled=True)
    near, *far = pack_q(routing, queries, send_kv, owners)
    groups = [list(range(half)), list(range(half, owners))]
    near = lax.all_to_all(near, "dp", split_axis=0, concat_axis=0, axis_index_groups=groups, tiled=True)
    label = parcels[:, :4].astype(jnp.float32).astype(jnp.int32)
    place, part = label[:, 2, 0], label[:, 3, 0]
    begin = (label[:, 0] * DIGIT + label[:, 1]).reshape(owners, LANES // cap, cap)
    slots = jnp.arange(blocks, dtype=jnp.int32)
    every = jnp.arange(owners, dtype=jnp.int32)
    chosen = place[None, :] == slots[:, None]
    source = jnp.sum(jnp.where(chosen, every[None, :], 0), axis=1)
    senders = jnp.concatenate([me // half * half + every[:half], me ^ every[half:]])
    places = jnp.sum(jnp.where(senders[:, None] == every[None, :], place[None, :], 0), axis=1)
    wanted = chosen[:, :, None] & (part[None, :, None] == jnp.arange(LANES // cap, dtype=jnp.int32))
    doc = jnp.sum(jnp.where(wanted[..., None], begin[None], 0), axis=(1, 2)).reshape(rows)

    split = jnp.concatenate([doc // DIGIT, doc % DIGIT]).astype(jnp.float32).astype(jnp.bfloat16).reshape(-1, LANES)
    split = jnp.pad(split, ((0, -split.shape[0] % LABEL_ROWS), (0, 0)))
    own_kv = place_kv(source, parcels, split, rows, cap)
    past_kv = lax.ppermute(own_kv, "ctx", [(0, 1)])[None] if columns == 2 else lax.all_gather(own_kv, "ctx")
    same, apart = digits(doc)
    own = (same, own_kv[: 2 * rows].reshape(rows, 2, LANES)[:, 0], apart, own_kv[: 2 * rows].reshape(rows, 2, LANES)[:, 1])
    past_doc = past_kv[:, 2 * rows :][:, : 2 * rows // LANES].reshape(-1, 2, rows).astype(jnp.float32).astype(jnp.int32)
    past_apart = digits(past_doc[:, 0] * DIGIT + past_doc[:, 1])[1]
    past_rows = past_kv[:, : 2 * rows].reshape(-1, rows, 2, LANES)
    past = (past_rows[:, :, 0], past_apart, past_rows[:, :, 1])

    ties = [None] * 3 + [parcels] * (half - 6) + [own_kv] * 2 + [past_kv]
    for index, tie in enumerate(ties):
        parcel = far[index] if tie is None else lax.optimization_barrier((far[index], tie))[0]
        far[index] = lax.ppermute(parcel, "dp", [(owner, owner ^ (half + index)) for owner in range(owners)])

    meta = jnp.concatenate([column[None], places])
    cuts = [0, half - 6, half - 3, half - 1, half]
    out = None
    for begin, end in zip(cuts[:-1], cuts[1:]):
        out = attend(
            meta, half + begin if begin else 0, None if begin else near, far[begin:end], own, past, out
        )
    return out


def solution(mesh):
    placed = (
        P(("dp", "ctx"), None),
        P(("dp", "ctx"), None, None, None),
        P(("dp", "ctx"), None),
        P(("dp", "ctx")),
    )
    return jax.shard_map(
        local, mesh=mesh, in_specs=placed, out_specs=P(("dp", "ctx"), None), check_vma=False
    )
```

```python
import functools
import math

import jax
import jax.numpy as jnp
from jax import lax
from jax.experimental import pallas as pl
from jax.experimental.pallas import tpu as pltpu
from jax.sharding import PartitionSpec as P

LANES = 128
LABEL_ROWS = 16
DIGIT = 64
TOGETHER = 4
APART = 16384.0
NEVER = -1e30
ANY = pl.BlockSpec(memory_space=pl.ANY)
VMEM = pl.BlockSpec(memory_space=pltpu.VMEM)
SMEM = pl.BlockSpec(memory_space=pltpu.SMEM)


def params(mib):
    return pltpu.CompilerParams(vmem_limit_bytes=mib * 1024 * 1024)


def hbm(*arrays):
    return [pltpu.with_memory_space_constraint(array, pltpu.HBM) for array in arrays]


def pack_kv(routing, documents, kv, owners, seq_len):
    rows = kv.shape[0] // 2
    cap = 2 * rows // owners
    blocks = rows // cap
    per_group = LANES // cap

    def kernel(routing_any, doc_any, kv_any, out_ref, routing_ref, doc_ref, kv_ref, label_ref, held_ref, in_sem, sem, label_sem):
        fetches = [
            pltpu.make_async_copy(source, target, in_sem.at[index])
            for index, (source, target) in enumerate(
                ((routing_any, routing_ref), (doc_any, doc_ref), (kv_any, kv_ref))
            )
        ]
        for fetch in fetches:
            fetch.start()
        fetches[0].wait()
        for slot in range(owners):
            held_ref[slot] = blocks
        for block in range(blocks):
            held_ref[routing_ref[0, block * cap]] = block
        fetches[1].wait()
        row_at = lax.broadcasted_iota(jnp.int32, (LABEL_ROWS, LANES), 0)
        label_ref[blocks] = jnp.full((LABEL_ROWS, LANES), 255.0, jnp.bfloat16)
        for block in range(blocks):
            group, part = divmod(block, per_group)
            begin = doc_ref[group : group + 1, :] - routing_ref[0, block * cap] * seq_len
            place = routing_ref[1, block * cap] // cap
            label = jnp.where(row_at == 0, begin // DIGIT, jnp.where(row_at == 1, begin % DIGIT, part))
            label = jnp.where(row_at == 2, place, label)
            label_ref[block] = label.astype(jnp.float32).astype(jnp.bfloat16)
        copies = [
            pltpu.make_async_copy(
                label_ref.at[held_ref[slot]], out_ref.at[slot, pl.ds(0, LABEL_ROWS)], label_sem.at[slot]
            )
            for slot in range(owners)
        ]
        for block in range(blocks):
            copies.append(
                pltpu.make_async_copy(
                    kv_ref.at[pl.ds(block * 2 * cap, 2 * cap)],
                    out_ref.at[routing_ref[0, block * cap], pl.ds(LABEL_ROWS, 2 * cap)],
                    sem.at[block],
                )
            )
        fetches[2].wait()
        for copy in copies:
            copy.start()
        for copy in copies:
            copy.wait()

    return pl.pallas_call(
        kernel,
        out_shape=pltpu.HBM((owners, LABEL_ROWS + 2 * cap, LANES), kv.dtype),
        in_specs=[ANY] * 3,
        out_specs=ANY,
        scratch_shapes=[
            pltpu.SMEM(routing.shape, jnp.int32),
            pltpu.VMEM(documents.shape, jnp.int32),
            pltpu.VMEM(kv.shape, kv.dtype),
            pltpu.VMEM((blocks + 1, LABEL_ROWS, LANES), jnp.bfloat16),
            pltpu.SMEM((owners,), jnp.int32),
            pltpu.SemaphoreType.DMA((3,)),
            pltpu.SemaphoreType.DMA((blocks,)),
            pltpu.SemaphoreType.DMA((owners,)),
        ],
        compiler_params=params(16),
        name="pack_kv",
    )(*hbm(routing, documents, kv))


def pack_q(routing, queries, earlier, owners):
    rows, width = queries.shape
    cap = 2 * rows // owners
    blocks = rows // cap
    half = owners // 2

    def kernel(routing_any, q_any, earlier_ref, near_ref, *rest):
        far_refs = rest[:half]
        routing_ref, q_ref, held_ref, in_sem, q_sem, sem = rest[half:]
        me = lax.axis_index("dp")
        fetch = pltpu.make_async_copy(routing_any, routing_ref, in_sem)
        fetch.start()
        fetch_q = pltpu.make_async_copy(q_any, q_ref, q_sem)
        fetch_q.start()
        fetch.wait()
        for slot in range(owners):
            held_ref[slot] = blocks
        for block in range(blocks):
            held_ref[routing_ref[0, block * cap]] = block
        copies = []
        for step in range(owners):
            slot = me ^ step
            block = held_ref[slot]
            q_rows = pl.ds(pl.multiple_of(jnp.minimum(block, blocks - 1) * cap, cap), cap)
            target = far_refs[step - half] if step >= half else near_ref.at[lax.rem(slot, half)]
            copies.append((block < blocks, pltpu.make_async_copy(q_ref.at[q_rows], target, sem.at[step])))
        fetch_q.wait()
        for held, copy in copies:
            pl.when(held)(copy.start)
        for held, copy in copies:
            pl.when(held)(copy.wait)

    return pl.pallas_call(
        kernel,
        out_shape=[
            pltpu.HBM((half, cap, width), queries.dtype),
            *[jax.ShapeDtypeStruct((cap, width), queries.dtype)] * half,
        ],
        in_specs=[ANY] * 3,
        out_specs=[ANY] * (1 + half),
        scratch_shapes=[
            pltpu.SMEM(routing.shape, jnp.int32),
            pltpu.VMEM(queries.shape, queries.dtype),
            pltpu.SMEM((owners,), jnp.int32),
            pltpu.SemaphoreType.DMA,
            pltpu.SemaphoreType.DMA,
            pltpu.SemaphoreType.DMA((owners,)),
        ],
        compiler_params=params(16),
        name="pack_q",
    )(*hbm(routing, queries, earlier))


def place_kv(source, parcels, begins, rows, cap):
    blocks = rows // cap

    def kernel(source_ref, in_ref, begin_ref, out_ref, sem):
        copies = [
            pltpu.make_async_copy(
                in_ref.at[source_ref[place], pl.ds(LABEL_ROWS, 2 * cap)],
                out_ref.at[pl.ds(place * 2 * cap, 2 * cap)],
                sem.at[place],
            )
            for place in range(blocks)
        ]
        copies.append(
            pltpu.make_async_copy(begin_ref, out_ref.at[pl.ds(2 * rows, begin_ref.shape[0])], sem.at[blocks])
        )
        for copy in copies:
            copy.start()
        for copy in copies:
            copy.wait()

    return pl.pallas_call(
        kernel,
        out_shape=jax.ShapeDtypeStruct((2 * rows + begins.shape[0], LANES), parcels.dtype),
        in_specs=[SMEM, ANY, ANY],
        out_specs=ANY,
        scratch_shapes=[pltpu.SemaphoreType.DMA((blocks + 1,))],
        compiler_params=params(16),
        name="place_kv",
    )(source, parcels, begins)


def attend(meta, first, near, far, own, past, out):
    rows = own[0].shape[0]
    cap, width = near.shape[1:] if far == [] else far[0].shape
    blocks = rows // cap
    heads = width // LANES
    half = rows // 2
    count = past[0].shape[0]
    slots = 0 if near is None else near.shape[0]
    parcels = slots + len(far)
    factor = math.log2(math.e) / math.sqrt(LANES)
    arrays = ([] if near is None else [near]) + far

    def kernel(meta_ref, qd_ref, ok_ref, od_ref, ov_ref, pk_ref, pd_ref, pv_ref, *rest):
        array_refs = rest[: len(arrays)]
        out_any, stage_ref, result_ref, sem = rest[-4:]

        def keys(k_ref, d_ref):
            return jnp.concatenate([k_ref, d_ref], axis=1)

        def values(v):
            return jnp.concatenate([v, jnp.ones(v.shape, v.dtype)], axis=1)

        def scores(tile_q, tile_k):
            return lax.dot_general(tile_q, tile_k, (((1,), (1,)), ((), ())), preferred_element_type=jnp.float32)

        def top(raw):
            return jnp.max(raw, axis=-1, keepdims=True)

        def mix(raw, peak, tile_v):
            weights = jnp.exp2((raw - peak) * factor).astype(jnp.bfloat16)
            return jnp.dot(weights, tile_v, preferred_element_type=jnp.float32)

        def place_of(index):
            return meta_ref[1 + first + index]

        def result_copy(index):
            at = pl.multiple_of(jnp.minimum(place_of(index), blocks - 1) * cap, cap)
            return pltpu.make_async_copy(result_ref.at[index], out_any.at[pl.ds(at, cap)], sem.at[index])

        def one_block(index, place, lower, with_past):
            block_q = stage_ref[index]
            same = qd_ref[pl.ds(pl.multiple_of(place * cap, cap), cap), :]
            same = jnp.concatenate([same] * TOGETHER, axis=0)
            row_at = lax.broadcasted_iota(jnp.int32, (cap, half), 0) + (place * cap - lower * half)
            seen = lax.broadcasted_iota(jnp.int32, (cap, half), 1) <= row_at
            last = pl.ds(lower * half, half)

            def causal(raw):
                return jnp.where(seen[None], raw.reshape(TOGETHER, cap, half), NEVER).reshape(TOGETHER * cap, half)

            tile_qs = []
            for begin in range(0, heads, TOGETHER):
                tiles = [block_q[:, head * LANES : (head + 1) * LANES] for head in range(begin, begin + TOGETHER)]
                tile_qs.append(jnp.concatenate([jnp.concatenate(tiles, axis=0), same], axis=1))
            raws = [[causal(scores(tile_q, keys(ok_ref[last], od_ref[last])))] for tile_q in tile_qs]
            tile_vs = [ov_ref[last]]
            if lower:
                for several, tile_q in zip(raws, tile_qs):
                    several.append(scores(tile_q, keys(ok_ref[:half], od_ref[:half])))
                tile_vs.append(ov_ref[:half])
            if with_past:
                for several, tile_q in zip(raws, tile_qs):
                    several.append(scores(tile_q, keys(pk_ref[0], pd_ref[0])))
                tile_vs.append(pv_ref[0])
            peaks = [functools.reduce(jnp.maximum, [top(raw) for raw in several]) for several in raws]
            mixes = [
                sum(mix(raw, peak, values(tile_v)) for raw, tile_v in zip(several, tile_vs))
                for several, peak in zip(raws, peaks)
            ]
            if count > 1:

                def step(earlier, state):
                    result = []
                    for (peak, mixed), tile_q in zip(state, tile_qs):
                        raw = scores(tile_q, keys(pk_ref[earlier], pd_ref[earlier]))
                        higher = jnp.maximum(peak, top(raw))
                        decay = jnp.exp2((peak - higher) * factor)
                        result.append((higher, mixed * decay + mix(raw, higher, values(pv_ref[earlier]))))
                    return result

                mixes = [mixed for _, mixed in lax.fori_loop(0, meta_ref[0], step, list(zip(peaks, mixes)))]
            for at, mixed in enumerate(mixes):
                result = (mixed[:, :LANES] / mixed[:, LANES:]).astype(jnp.bfloat16)
                for head in range(TOGETHER):
                    column = (at * TOGETHER + head) * LANES
                    result_ref[index, :, column : column + LANES] = result[head * cap : (head + 1) * cap]

        def body(index, carry):
            place = place_of(index)
            for lower in (0, 1):
                here = (place < blocks) & (place >= blocks // 2) if lower else place < blocks // 2
                if count > 1:
                    pl.when(here)(functools.partial(one_block, index, place, lower, False))
                else:
                    for column in (0, 1):
                        pl.when(here & (meta_ref[0] == column))(
                            functools.partial(one_block, index, place, lower, column == 1)
                        )
            pl.when(place < blocks)(result_copy(index).start)
            return carry

        for index in range(parcels):

            @pl.when(place_of(index) < blocks)
            def _():
                stage_ref[index] = array_refs[0][index] if index < slots else array_refs[index - slots + (slots > 0)][...]

        lax.fori_loop(0, parcels, body, 0)
        for index in range(parcels):
            pl.when(place_of(index) < blocks)(result_copy(index).wait)

    operands = [meta, *own, *past, *arrays]
    specs = [SMEM] + [VMEM] * (len(operands) - 1)
    aliases = {}
    if out is not None:
        aliases = {len(operands): 0}
        operands.append(out)
        specs.append(ANY)
    area = max(1, parcels // 2) * heads * cap * (count + 1) * rows
    return pl.pallas_call(
        kernel,
        out_shape=jax.ShapeDtypeStruct((rows, width), jnp.bfloat16),
        in_specs=specs,
        out_specs=ANY,
        input_output_aliases=aliases,
        scratch_shapes=[
            pltpu.VMEM((parcels, cap, width), jnp.bfloat16),
            pltpu.VMEM((parcels, cap, width), jnp.bfloat16),
            pltpu.SemaphoreType.DMA((parcels,)),
        ],
        compiler_params=params(28),
        cost_estimate=pl.CostEstimate(
            flops=8 * area * LANES, bytes_accessed=4 * parcels * cap * width, transcendentals=area
        ),
        name="attend",
    )(*operands)


def digits(begin):
    lane = jnp.arange(LANES, dtype=jnp.int32)
    digit = jnp.where(lane < DIGIT, begin[..., None] // DIGIT, begin[..., None] % DIGIT)
    hit = digit == lane % DIGIT
    return jnp.where(hit, 1.0, 0.0).astype(jnp.bfloat16), jnp.where(hit, 0.0, -APART).astype(jnp.bfloat16)


def local(queries, keys_values, routing, documents):
    rows, width = queries.shape
    owners = lax.axis_size("dp")
    columns = lax.axis_size("ctx")
    kv_heads, pair, head_dim = keys_values.shape[1:]
    assert kv_heads == 1 and pair == 2 and head_dim == LANES
    cap = 2 * rows // owners
    blocks = rows // cap
    seq_len = rows * columns
    assert seq_len <= DIGIT * DIGIT
    half = owners // 2
    assert owners & (owners - 1) == 0
    column = lax.axis_index("ctx")
    me = lax.axis_index("dp")

    routing = routing.T
    send_kv = pack_kv(routing, documents.reshape(-1, LANES), keys_values.reshape(2 * rows, LANES), owners, seq_len)
    parcels = lax.all_to_all(send_kv, "dp", split_axis=0, concat_axis=0, tiled=True)
    near, *far = pack_q(routing, queries, send_kv, owners)
    groups = [list(range(half)), list(range(half, owners))]
    near = lax.all_to_all(near, "dp", split_axis=0, concat_axis=0, axis_index_groups=groups, tiled=True)
    label = parcels[:, :4].astype(jnp.float32).astype(jnp.int32)
    place, part = label[:, 2, 0], label[:, 3, 0]
    begin = (label[:, 0] * DIGIT + label[:, 1]).reshape(owners, LANES // cap, cap)
    slots = jnp.arange(blocks, dtype=jnp.int32)
    every = jnp.arange(owners, dtype=jnp.int32)
    chosen = place[None, :] == slots[:, None]
    source = jnp.sum(jnp.where(chosen, every[None, :], 0), axis=1)
    senders = jnp.concatenate([me // half * half + every[:half], me ^ every[half:]])
    places = jnp.sum(jnp.where(senders[:, None] == every[None, :], place[None, :], 0), axis=1)
    wanted = chosen[:, :, None] & (part[None, :, None] == jnp.arange(LANES // cap, dtype=jnp.int32))
    doc = jnp.sum(jnp.where(wanted[..., None], begin[None], 0), axis=(1, 2)).reshape(rows)

    split = jnp.concatenate([doc // DIGIT, doc % DIGIT]).astype(jnp.float32).astype(jnp.bfloat16).reshape(-1, LANES)
    split = jnp.pad(split, ((0, -split.shape[0] % LABEL_ROWS), (0, 0)))
    own_kv = place_kv(source, parcels, split, rows, cap)
    past_kv = lax.ppermute(own_kv, "ctx", [(0, 1)])[None] if columns == 2 else lax.all_gather(own_kv, "ctx")
    same, apart = digits(doc)
    own = (same, own_kv[: 2 * rows].reshape(rows, 2, LANES)[:, 0], apart, own_kv[: 2 * rows].reshape(rows, 2, LANES)[:, 1])
    past_doc = past_kv[:, 2 * rows :][:, : 2 * rows // LANES].reshape(-1, 2, rows).astype(jnp.float32).astype(jnp.int32)
    past_apart = digits(past_doc[:, 0] * DIGIT + past_doc[:, 1])[1]
    past_rows = past_kv[:, : 2 * rows].reshape(-1, rows, 2, LANES)
    past = (past_rows[:, :, 0], past_apart, past_rows[:, :, 1])

    sent, far = far, []
    for index, parcel in enumerate(sent):
        if index >= 3:
            ties = [far[index - 3], own_kv] if index < half - 2 else [past_kv] if index < half - 1 else [far[index - 4], past_kv]
            parcel = lax.optimization_barrier((parcel, *ties))[0]
        far.append(lax.ppermute(parcel, "dp", [(owner, owner ^ (half + index)) for owner in range(owners)]))

    meta = jnp.concatenate([column[None], places])
    cuts = [0, half - 5, half - 3, None, half - 3, half - 1, half]
    out = None
    for begin, end in zip(cuts[:-1], cuts[1:]):
        if begin is None:
            out = attend(meta, 0, near, [], own, past, out)
        elif end is not None:
            out = attend(meta, half + begin, None, far[begin:end], own, past, out)
    return out


def solution(mesh):
    placed = (
        P(("dp", "ctx"), None),
        P(("dp", "ctx"), None, None, None),
        P(("dp", "ctx"), None),
        P(("dp", "ctx")),
    )
    return jax.shard_map(
        local, mesh=mesh, in_specs=placed, out_specs=P(("dp", "ctx"), None), check_vma=False
    )
```

```python
import functools
import math

import jax
import jax.numpy as jnp
from jax import lax
from jax.experimental import pallas as pl
from jax.experimental.pallas import tpu as pltpu
from jax.sharding import PartitionSpec as P

LANES = 128
LABEL_ROWS = 16
DIGIT = 64
TOGETHER = 4
APART = 16384.0
NEVER = -1e30
ANY = pl.BlockSpec(memory_space=pl.ANY)
VMEM = pl.BlockSpec(memory_space=pltpu.VMEM)
SMEM = pl.BlockSpec(memory_space=pltpu.SMEM)


def params(mib):
    return pltpu.CompilerParams(vmem_limit_bytes=mib * 1024 * 1024)


def hbm(*arrays):
    return [pltpu.with_memory_space_constraint(array, pltpu.HBM) for array in arrays]


def pack_kv(routing, documents, kv, owners, seq_len):
    rows = kv.shape[0] // 2
    cap = 2 * rows // owners
    blocks = rows // cap
    per_group = LANES // cap

    def kernel(routing_any, doc_any, kv_any, out_ref, routing_ref, doc_ref, kv_ref, label_ref, held_ref, in_sem, sem, label_sem):
        fetches = [
            pltpu.make_async_copy(source, target, in_sem.at[index])
            for index, (source, target) in enumerate(
                ((routing_any, routing_ref), (doc_any, doc_ref), (kv_any, kv_ref))
            )
        ]
        for fetch in fetches:
            fetch.start()
        fetches[0].wait()
        for slot in range(owners):
            held_ref[slot] = blocks
        for block in range(blocks):
            held_ref[routing_ref[0, block * cap]] = block
        fetches[1].wait()
        row_at = lax.broadcasted_iota(jnp.int32, (LABEL_ROWS, LANES), 0)
        label_ref[blocks] = jnp.full((LABEL_ROWS, LANES), 255.0, jnp.bfloat16)
        for block in range(blocks):
            group, part = divmod(block, per_group)
            begin = doc_ref[group : group + 1, :] - routing_ref[0, block * cap] * seq_len
            place = routing_ref[1, block * cap] // cap
            label = jnp.where(row_at == 0, begin // DIGIT, jnp.where(row_at == 1, begin % DIGIT, part))
            label = jnp.where(row_at == 2, place, label)
            label_ref[block] = label.astype(jnp.float32).astype(jnp.bfloat16)
        copies = [
            pltpu.make_async_copy(
                label_ref.at[held_ref[slot]], out_ref.at[slot, pl.ds(0, LABEL_ROWS)], label_sem.at[slot]
            )
            for slot in range(owners)
        ]
        for block in range(blocks):
            copies.append(
                pltpu.make_async_copy(
                    kv_ref.at[pl.ds(block * 2 * cap, 2 * cap)],
                    out_ref.at[routing_ref[0, block * cap], pl.ds(LABEL_ROWS, 2 * cap)],
                    sem.at[block],
                )
            )
        fetches[2].wait()
        for copy in copies:
            copy.start()
        for copy in copies:
            copy.wait()

    return pl.pallas_call(
        kernel,
        out_shape=pltpu.HBM((owners, LABEL_ROWS + 2 * cap, LANES), kv.dtype),
        in_specs=[ANY] * 3,
        out_specs=ANY,
        scratch_shapes=[
            pltpu.SMEM(routing.shape, jnp.int32),
            pltpu.VMEM(documents.shape, jnp.int32),
            pltpu.VMEM(kv.shape, kv.dtype),
            pltpu.VMEM((blocks + 1, LABEL_ROWS, LANES), jnp.bfloat16),
            pltpu.SMEM((owners,), jnp.int32),
            pltpu.SemaphoreType.DMA((3,)),
            pltpu.SemaphoreType.DMA((blocks,)),
            pltpu.SemaphoreType.DMA((owners,)),
        ],
        compiler_params=params(16),
        name="pack_kv",
    )(*hbm(routing, documents, kv))


def pack_q(routing, queries, earlier, owners):
    rows, width = queries.shape
    cap = 2 * rows // owners
    blocks = rows // cap
    half = owners // 2

    def kernel(routing_any, q_any, earlier_ref, near_ref, *rest):
        far_refs = rest[:half]
        routing_ref, q_ref, held_ref, in_sem, q_sem, sem = rest[half:]
        me = lax.axis_index("dp")
        fetch = pltpu.make_async_copy(routing_any, routing_ref, in_sem)
        fetch.start()
        fetch_q = pltpu.make_async_copy(q_any, q_ref, q_sem)
        fetch_q.start()
        fetch.wait()
        for slot in range(owners):
            held_ref[slot] = blocks
        for block in range(blocks):
            held_ref[routing_ref[0, block * cap]] = block
        copies = []
        for step in range(owners):
            slot = me ^ step
            block = held_ref[slot]
            q_rows = pl.ds(pl.multiple_of(jnp.minimum(block, blocks - 1) * cap, cap), cap)
            target = far_refs[step - half] if step >= half else near_ref.at[lax.rem(slot, half)]
            copies.append((block < blocks, pltpu.make_async_copy(q_ref.at[q_rows], target, sem.at[step])))
        fetch_q.wait()
        for held, copy in copies:
            pl.when(held)(copy.start)
        for held, copy in copies:
            pl.when(held)(copy.wait)

    return pl.pallas_call(
        kernel,
        out_shape=[
            pltpu.HBM((half, cap, width), queries.dtype),
            *[jax.ShapeDtypeStruct((cap, width), queries.dtype)] * half,
        ],
        in_specs=[ANY] * 3,
        out_specs=[ANY] * (1 + half),
        scratch_shapes=[
            pltpu.SMEM(routing.shape, jnp.int32),
            pltpu.VMEM(queries.shape, queries.dtype),
            pltpu.SMEM((owners,), jnp.int32),
            pltpu.SemaphoreType.DMA,
            pltpu.SemaphoreType.DMA,
            pltpu.SemaphoreType.DMA((owners,)),
        ],
        compiler_params=params(16),
        name="pack_q",
    )(*hbm(routing, queries, earlier))


def place_kv(source, parcels, begins, rows, cap):
    blocks = rows // cap

    def kernel(source_ref, in_ref, begin_ref, out_ref, sem):
        copies = [
            pltpu.make_async_copy(
                in_ref.at[source_ref[place], pl.ds(LABEL_ROWS, 2 * cap)],
                out_ref.at[pl.ds(place * 2 * cap, 2 * cap)],
                sem.at[place],
            )
            for place in range(blocks)
        ]
        copies.append(
            pltpu.make_async_copy(begin_ref, out_ref.at[pl.ds(2 * rows, begin_ref.shape[0])], sem.at[blocks])
        )
        for copy in copies:
            copy.start()
        for copy in copies:
            copy.wait()

    return pl.pallas_call(
        kernel,
        out_shape=jax.ShapeDtypeStruct((2 * rows + begins.shape[0], LANES), parcels.dtype),
        in_specs=[SMEM, ANY, ANY],
        out_specs=ANY,
        scratch_shapes=[pltpu.SemaphoreType.DMA((blocks + 1,))],
        compiler_params=params(16),
        name="place_kv",
    )(source, parcels, begins)


def attend(meta, first, near, far, own, past, out):
    rows = own[0].shape[0]
    cap, width = near.shape[1:] if far == [] else far[0].shape
    blocks = rows // cap
    heads = width // LANES
    half = rows // 2
    count = past[0].shape[0]
    slots = 0 if near is None else near.shape[0]
    parcels = slots + len(far)
    factor = math.log2(math.e) / math.sqrt(LANES)
    arrays = ([] if near is None else [near]) + far

    def kernel(meta_ref, qd_ref, ok_ref, od_ref, ov_ref, pk_ref, pd_ref, pv_ref, *rest):
        array_refs = rest[: len(arrays)]
        out_any, token_ref, stage_ref, result_ref, sem = rest[-5:]
        token_ref[...] = jnp.zeros_like(token_ref)

        def keys(k_ref, d_ref):
            return jnp.concatenate([k_ref, d_ref], axis=1)

        def values(v):
            return jnp.concatenate([v, jnp.ones(v.shape, v.dtype)], axis=1)

        def scores(tile_q, tile_k):
            return lax.dot_general(tile_q, tile_k, (((1,), (1,)), ((), ())), preferred_element_type=jnp.float32)

        def top(raw):
            return jnp.max(raw, axis=-1, keepdims=True)

        def mix(raw, peak, tile_v):
            weights = jnp.exp2((raw - peak) * factor).astype(jnp.bfloat16)
            return jnp.dot(weights, tile_v, preferred_element_type=jnp.float32)

        def place_of(index):
            return meta_ref[1 + first + index]

        def result_copy(index):
            at = pl.multiple_of(jnp.minimum(place_of(index), blocks - 1) * cap, cap)
            return pltpu.make_async_copy(result_ref.at[index], out_any.at[pl.ds(at, cap)], sem.at[index])

        def one_block(index, place, lower, with_past):
            block_q = stage_ref[index]
            same = qd_ref[pl.ds(pl.multiple_of(place * cap, cap), cap), :]
            same = jnp.concatenate([same] * TOGETHER, axis=0)
            row_at = lax.broadcasted_iota(jnp.int32, (cap, half), 0) + (place * cap - lower * half)
            seen = lax.broadcasted_iota(jnp.int32, (cap, half), 1) <= row_at
            last = pl.ds(lower * half, half)

            def causal(raw):
                return jnp.where(seen[None], raw.reshape(TOGETHER, cap, half), NEVER).reshape(TOGETHER * cap, half)

            tile_qs = []
            for begin in range(0, heads, TOGETHER):
                tiles = [block_q[:, head * LANES : (head + 1) * LANES] for head in range(begin, begin + TOGETHER)]
                tile_qs.append(jnp.concatenate([jnp.concatenate(tiles, axis=0), same], axis=1))
            raws = [[causal(scores(tile_q, keys(ok_ref[last], od_ref[last])))] for tile_q in tile_qs]
            tile_vs = [ov_ref[last]]
            if lower:
                for several, tile_q in zip(raws, tile_qs):
                    several.append(scores(tile_q, keys(ok_ref[:half], od_ref[:half])))
                tile_vs.append(ov_ref[:half])
            if with_past:
                for several, tile_q in zip(raws, tile_qs):
                    several.append(scores(tile_q, keys(pk_ref[0], pd_ref[0])))
                tile_vs.append(pv_ref[0])
            peaks = [functools.reduce(jnp.maximum, [top(raw) for raw in several]) for several in raws]
            mixes = [
                sum(mix(raw, peak, values(tile_v)) for raw, tile_v in zip(several, tile_vs))
                for several, peak in zip(raws, peaks)
            ]
            if count > 1:

                def step(earlier, state):
                    result = []
                    for (peak, mixed), tile_q in zip(state, tile_qs):
                        raw = scores(tile_q, keys(pk_ref[earlier], pd_ref[earlier]))
                        higher = jnp.maximum(peak, top(raw))
                        decay = jnp.exp2((peak - higher) * factor)
                        result.append((higher, mixed * decay + mix(raw, higher, values(pv_ref[earlier]))))
                    return result

                mixes = [mixed for _, mixed in lax.fori_loop(0, meta_ref[0], step, list(zip(peaks, mixes)))]
            for at, mixed in enumerate(mixes):
                result = (mixed[:, :LANES] / mixed[:, LANES:]).astype(jnp.bfloat16)
                for head in range(TOGETHER):
                    column = (at * TOGETHER + head) * LANES
                    result_ref[index, :, column : column + LANES] = result[head * cap : (head + 1) * cap]

        def body(index, carry):
            place = place_of(index)
            for lower in (0, 1):
                here = (place < blocks) & (place >= blocks // 2) if lower else place < blocks // 2
                if count > 1:
                    pl.when(here)(functools.partial(one_block, index, place, lower, False))
                else:
                    for column in (0, 1):
                        pl.when(here & (meta_ref[0] == column))(
                            functools.partial(one_block, index, place, lower, column == 1)
                        )
            pl.when(place < blocks)(result_copy(index).start)
            return carry

        for index in range(parcels):

            @pl.when(place_of(index) < blocks)
            def _():
                stage_ref[index] = array_refs[0][index] if index < slots else array_refs[index - slots + (slots > 0)][...]

        lax.fori_loop(0, parcels, body, 0)
        for index in range(parcels):
            pl.when(place_of(index) < blocks)(result_copy(index).wait)

    operands = [meta, *own, *past, *arrays]
    specs = [SMEM] + [VMEM] * (len(operands) - 1)
    aliases = {}
    if out is not None:
        aliases = {len(operands): 0}
        operands.append(out)
        specs.append(ANY)
    area = max(1, parcels // 2) * heads * cap * (count + 1) * rows
    return pl.pallas_call(
        kernel,
        out_shape=[
            jax.ShapeDtypeStruct((rows, width), jnp.bfloat16),
            jax.ShapeDtypeStruct((8, LANES), jnp.int32),
        ],
        in_specs=specs,
        out_specs=[ANY, VMEM],
        input_output_aliases=aliases,
        scratch_shapes=[
            pltpu.VMEM((parcels, cap, width), jnp.bfloat16),
            pltpu.VMEM((parcels, cap, width), jnp.bfloat16),
            pltpu.SemaphoreType.DMA((parcels,)),
        ],
        compiler_params=params(28),
        cost_estimate=pl.CostEstimate(
            flops=8 * area * LANES, bytes_accessed=4 * parcels * cap * width, transcendentals=area
        ),
        name="attend",
    )(*operands)


def digits(begin):
    lane = jnp.arange(LANES, dtype=jnp.int32)
    digit = jnp.where(lane < DIGIT, begin[..., None] // DIGIT, begin[..., None] % DIGIT)
    hit = digit == lane % DIGIT
    return jnp.where(hit, 1.0, 0.0).astype(jnp.bfloat16), jnp.where(hit, 0.0, -APART).astype(jnp.bfloat16)


def local(queries, keys_values, routing, documents):
    rows, width = queries.shape
    owners = lax.axis_size("dp")
    columns = lax.axis_size("ctx")
    kv_heads, pair, head_dim = keys_values.shape[1:]
    assert kv_heads == 1 and pair == 2 and head_dim == LANES
    cap = 2 * rows // owners
    blocks = rows // cap
    seq_len = rows * columns
    assert seq_len <= DIGIT * DIGIT
    half = owners // 2
    assert owners & (owners - 1) == 0
    column = lax.axis_index("ctx")
    me = lax.axis_index("dp")

    routing = routing.T
    send_kv = pack_kv(routing, documents.reshape(-1, LANES), keys_values.reshape(2 * rows, LANES), owners, seq_len)
    parcels = lax.all_to_all(send_kv, "dp", split_axis=0, concat_axis=0, tiled=True)
    near, *far = pack_q(routing, queries, send_kv, owners)
    groups = [list(range(half)), list(range(half, owners))]
    near = lax.all_to_all(near, "dp", split_axis=0, concat_axis=0, axis_index_groups=groups, tiled=True)
    label = parcels[:, :4].astype(jnp.float32).astype(jnp.int32)
    place, part = label[:, 2, 0], label[:, 3, 0]
    begin = (label[:, 0] * DIGIT + label[:, 1]).reshape(owners, LANES // cap, cap)
    slots = jnp.arange(blocks, dtype=jnp.int32)
    every = jnp.arange(owners, dtype=jnp.int32)
    chosen = place[None, :] == slots[:, None]
    source = jnp.sum(jnp.where(chosen, every[None, :], 0), axis=1)
    senders = jnp.concatenate([me // half * half + every[:half], me ^ every[half:]])
    places = jnp.sum(jnp.where(senders[:, None] == every[None, :], place[None, :], 0), axis=1)
    wanted = chosen[:, :, None] & (part[None, :, None] == jnp.arange(LANES // cap, dtype=jnp.int32))
    doc = jnp.sum(jnp.where(wanted[..., None], begin[None], 0), axis=(1, 2)).reshape(rows)

    split = jnp.concatenate([doc // DIGIT, doc % DIGIT]).astype(jnp.float32).astype(jnp.bfloat16).reshape(-1, LANES)
    split = jnp.pad(split, ((0, -split.shape[0] % LABEL_ROWS), (0, 0)))
    own_kv = place_kv(source, parcels, split, rows, cap)
    past_kv = lax.ppermute(own_kv, "ctx", [(0, 1)])[None] if columns == 2 else lax.all_gather(own_kv, "ctx")
    same, apart = digits(doc)
    own = (same, own_kv[: 2 * rows].reshape(rows, 2, LANES)[:, 0], apart, own_kv[: 2 * rows].reshape(rows, 2, LANES)[:, 1])
    past_doc = past_kv[:, 2 * rows :][:, : 2 * rows // LANES].reshape(-1, 2, rows).astype(jnp.float32).astype(jnp.int32)
    past_apart = digits(past_doc[:, 0] * DIGIT + past_doc[:, 1])[1]
    past_rows = past_kv[:, : 2 * rows].reshape(-1, rows, 2, LANES)
    past = (past_rows[:, :, 0], past_apart, past_rows[:, :, 1])

    meta = jnp.concatenate([column[None], places])
    sent, far = far, []
    out = token = None
    for index, parcel in enumerate(sent):
        if index == half - 2:
            out, token = attend(meta, half, None, far[: half - 5], own, past, None)
        if index >= 3:
            ties = (token,) if index >= half - 2 else (far[index - 3], own_kv if index > 3 else parcels)
            parcel = lax.optimization_barrier((parcel, *ties))[0]
        far.append(lax.ppermute(parcel, "dp", [(owner, owner ^ (half + index)) for owner in range(owners)]))
    out, _ = attend(meta, 0, near, [], own, past, out)
    for begin, end in ((half - 5, half - 2), (half - 2, half)):
        out, _ = attend(meta, half + begin, None, far[begin:end], own, past, out)
    return out


def solution(mesh):
    placed = (
        P(("dp", "ctx"), None),
        P(("dp", "ctx"), None, None, None),
        P(("dp", "ctx"), None),
        P(("dp", "ctx")),
    )
    return jax.shard_map(
        local, mesh=mesh, in_specs=placed, out_specs=P(("dp", "ctx"), None), check_vma=False
    )
```

```python
import functools
import math

import jax
import jax.numpy as jnp
from jax import lax
from jax.experimental import pallas as pl
from jax.experimental.pallas import tpu as pltpu
from jax.sharding import PartitionSpec as P

LANES = 128
LABEL_ROWS = 16
DIGIT = 64
TOGETHER = 4
APART = 16384.0
NEVER = -1e30
ANY = pl.BlockSpec(memory_space=pl.ANY)
VMEM = pl.BlockSpec(memory_space=pltpu.VMEM)
SMEM = pl.BlockSpec(memory_space=pltpu.SMEM)


def params(mib):
    return pltpu.CompilerParams(vmem_limit_bytes=mib * 1024 * 1024)


def hbm(*arrays):
    return [pltpu.with_memory_space_constraint(array, pltpu.HBM) for array in arrays]


def pack_kv(routing, documents, kv, owners, seq_len):
    rows = kv.shape[0] // 2
    cap = 2 * rows // owners
    blocks = rows // cap
    per_group = LANES // cap

    def kernel(routing_any, doc_any, kv_any, out_ref, routing_ref, doc_ref, kv_ref, label_ref, held_ref, in_sem, sem, label_sem):
        fetches = [
            pltpu.make_async_copy(source, target, in_sem.at[index])
            for index, (source, target) in enumerate(
                ((routing_any, routing_ref), (doc_any, doc_ref), (kv_any, kv_ref))
            )
        ]
        for fetch in fetches:
            fetch.start()
        fetches[0].wait()
        for slot in range(owners):
            held_ref[slot] = blocks
        for block in range(blocks):
            held_ref[routing_ref[0, block * cap]] = block
        fetches[1].wait()
        row_at = lax.broadcasted_iota(jnp.int32, (LABEL_ROWS, LANES), 0)
        label_ref[blocks] = jnp.full((LABEL_ROWS, LANES), 255.0, jnp.bfloat16)
        for block in range(blocks):
            group, part = divmod(block, per_group)
            begin = doc_ref[group : group + 1, :] - routing_ref[0, block * cap] * seq_len
            place = routing_ref[1, block * cap] // cap
            label = jnp.where(row_at == 0, begin // DIGIT, jnp.where(row_at == 1, begin % DIGIT, part))
            label = jnp.where(row_at == 2, place, label)
            label_ref[block] = label.astype(jnp.float32).astype(jnp.bfloat16)
        copies = [
            pltpu.make_async_copy(
                label_ref.at[held_ref[slot]], out_ref.at[slot, pl.ds(0, LABEL_ROWS)], label_sem.at[slot]
            )
            for slot in range(owners)
        ]
        for block in range(blocks):
            copies.append(
                pltpu.make_async_copy(
                    kv_ref.at[pl.ds(block * 2 * cap, 2 * cap)],
                    out_ref.at[routing_ref[0, block * cap], pl.ds(LABEL_ROWS, 2 * cap)],
                    sem.at[block],
                )
            )
        fetches[2].wait()
        for copy in copies:
            copy.start()
        for copy in copies:
            copy.wait()

    return pl.pallas_call(
        kernel,
        out_shape=pltpu.HBM((owners, LABEL_ROWS + 2 * cap, LANES), kv.dtype),
        in_specs=[ANY] * 3,
        out_specs=ANY,
        scratch_shapes=[
            pltpu.SMEM(routing.shape, jnp.int32),
            pltpu.VMEM(documents.shape, jnp.int32),
            pltpu.VMEM(kv.shape, kv.dtype),
            pltpu.VMEM((blocks + 1, LABEL_ROWS, LANES), jnp.bfloat16),
            pltpu.SMEM((owners,), jnp.int32),
            pltpu.SemaphoreType.DMA((3,)),
            pltpu.SemaphoreType.DMA((blocks,)),
            pltpu.SemaphoreType.DMA((owners,)),
        ],
        compiler_params=params(16),
        name="pack_kv",
    )(*hbm(routing, documents, kv))


def pack_q(routing, queries, earlier, owners):
    rows, width = queries.shape
    cap = 2 * rows // owners
    blocks = rows // cap
    half = owners // 2

    def kernel(routing_any, q_any, earlier_ref, near_ref, *rest):
        far_refs = rest[:half]
        routing_ref, q_ref, held_ref, in_sem, q_sem, sem = rest[half:]
        me = lax.axis_index("dp")
        fetch = pltpu.make_async_copy(routing_any, routing_ref, in_sem)
        fetch.start()
        fetch_q = pltpu.make_async_copy(q_any, q_ref, q_sem)
        fetch_q.start()
        fetch.wait()
        for slot in range(owners):
            held_ref[slot] = blocks
        for block in range(blocks):
            held_ref[routing_ref[0, block * cap]] = block
        copies = []
        for step in range(owners):
            slot = me ^ step
            block = held_ref[slot]
            q_rows = pl.ds(pl.multiple_of(jnp.minimum(block, blocks - 1) * cap, cap), cap)
            target = far_refs[step - half] if step >= half else near_ref.at[lax.rem(slot, half)]
            copies.append((block < blocks, pltpu.make_async_copy(q_ref.at[q_rows], target, sem.at[step])))
        fetch_q.wait()
        for held, copy in copies:
            pl.when(held)(copy.start)
        for held, copy in copies:
            pl.when(held)(copy.wait)

    return pl.pallas_call(
        kernel,
        out_shape=[
            pltpu.HBM((half, cap, width), queries.dtype),
            *[jax.ShapeDtypeStruct((cap, width), queries.dtype)] * half,
        ],
        in_specs=[ANY] * 3,
        out_specs=[ANY] * (1 + half),
        scratch_shapes=[
            pltpu.SMEM(routing.shape, jnp.int32),
            pltpu.VMEM(queries.shape, queries.dtype),
            pltpu.SMEM((owners,), jnp.int32),
            pltpu.SemaphoreType.DMA,
            pltpu.SemaphoreType.DMA,
            pltpu.SemaphoreType.DMA((owners,)),
        ],
        compiler_params=params(16),
        name="pack_q",
    )(*hbm(routing, queries, earlier))


def place_kv(source, parcels, begins, rows, cap):
    blocks = rows // cap

    def kernel(source_ref, in_ref, begin_ref, out_ref, sem):
        copies = [
            pltpu.make_async_copy(
                in_ref.at[source_ref[place], pl.ds(LABEL_ROWS, 2 * cap)],
                out_ref.at[pl.ds(place * 2 * cap, 2 * cap)],
                sem.at[place],
            )
            for place in range(blocks)
        ]
        copies.append(
            pltpu.make_async_copy(begin_ref, out_ref.at[pl.ds(2 * rows, begin_ref.shape[0])], sem.at[blocks])
        )
        for copy in copies:
            copy.start()
        for copy in copies:
            copy.wait()

    return pl.pallas_call(
        kernel,
        out_shape=jax.ShapeDtypeStruct((2 * rows + begins.shape[0], LANES), parcels.dtype),
        in_specs=[SMEM, ANY, ANY],
        out_specs=ANY,
        scratch_shapes=[pltpu.SemaphoreType.DMA((blocks + 1,))],
        compiler_params=params(16),
        name="place_kv",
    )(source, parcels, begins)


def attend(meta, first, near, far, own, past, out):
    rows = own[0].shape[0]
    cap, width = far[0].shape
    blocks = rows // cap
    heads = width // LANES
    half = rows // 2
    count = past[0].shape[0]
    slots = 0 if near is None else near.shape[0]
    parcels = slots + len(far)
    lows_at = meta.shape[0] - blocks
    factor = math.log2(math.e) / math.sqrt(LANES)
    arrays = ([] if near is None else [near]) + far

    def kernel(meta_ref, qd_ref, ok_ref, od_ref, ov_ref, pk_ref, pd_ref, pv_ref, *rest):
        array_refs = rest[: len(arrays)]
        out_any, stage_ref, result_ref, sem = rest[-4:]

        def keys(k_ref, d_ref):
            return jnp.concatenate([k_ref, d_ref], axis=1)

        def values(v):
            return jnp.concatenate([v, jnp.ones(v.shape, v.dtype)], axis=1)

        def scores(tile_q, tile_k):
            return lax.dot_general(tile_q, tile_k, (((1,), (1,)), ((), ())), preferred_element_type=jnp.float32)

        def top(raw):
            return jnp.max(raw, axis=-1, keepdims=True)

        def mix(raw, peak, tile_v):
            weights = jnp.exp2((raw - peak) * factor).astype(jnp.bfloat16)
            return jnp.dot(weights, tile_v, preferred_element_type=jnp.float32)

        def place_of(index):
            return meta_ref[1 + first + index]

        def low_of(place):
            return meta_ref[lows_at + jnp.minimum(place, blocks - 1)]

        def result_copy(index):
            at = pl.multiple_of(jnp.minimum(place_of(index), blocks - 1) * cap, cap)
            return pltpu.make_async_copy(result_ref.at[index], out_any.at[pl.ds(at, cap)], sem.at[index])

        def one_block(index, place, lower, with_low, with_past):
            block_q = stage_ref[index]
            same = qd_ref[pl.ds(pl.multiple_of(place * cap, cap), cap), :]
            same = jnp.concatenate([same] * TOGETHER, axis=0)
            row_at = lax.broadcasted_iota(jnp.int32, (cap, half), 0) + (place * cap - lower * half)
            seen = lax.broadcasted_iota(jnp.int32, (cap, half), 1) <= row_at
            last = pl.ds(lower * half, half)

            def causal(raw):
                return jnp.where(seen[None], raw.reshape(TOGETHER, cap, half), NEVER).reshape(TOGETHER * cap, half)

            tile_qs = []
            for begin in range(0, heads, TOGETHER):
                tiles = [block_q[:, head * LANES : (head + 1) * LANES] for head in range(begin, begin + TOGETHER)]
                tile_qs.append(jnp.concatenate([jnp.concatenate(tiles, axis=0), same], axis=1))
            raws = [[causal(scores(tile_q, keys(ok_ref[last], od_ref[last])))] for tile_q in tile_qs]
            tile_vs = [ov_ref[last]]
            if with_low:
                for several, tile_q in zip(raws, tile_qs):
                    several.append(scores(tile_q, keys(ok_ref[:half], od_ref[:half])))
                tile_vs.append(ov_ref[:half])
            if with_past:
                for several, tile_q in zip(raws, tile_qs):
                    several.append(scores(tile_q, keys(pk_ref[0], pd_ref[0])))
                tile_vs.append(pv_ref[0])
            peaks = [functools.reduce(jnp.maximum, [top(raw) for raw in several]) for several in raws]
            mixes = [
                sum(mix(raw, peak, values(tile_v)) for raw, tile_v in zip(several, tile_vs))
                for several, peak in zip(raws, peaks)
            ]
            if count > 1:

                def step(earlier, state):
                    result = []
                    for (peak, mixed), tile_q in zip(state, tile_qs):
                        raw = scores(tile_q, keys(pk_ref[earlier], pd_ref[earlier]))
                        higher = jnp.maximum(peak, top(raw))
                        decay = jnp.exp2((peak - higher) * factor)
                        result.append((higher, mixed * decay + mix(raw, higher, values(pv_ref[earlier]))))
                    return result

                least = jnp.maximum(low_of(place) + meta_ref[0] * rows, 0) // rows
                mixes = [mixed for _, mixed in lax.fori_loop(least, meta_ref[0], step, list(zip(peaks, mixes)))]
            for at, mixed in enumerate(mixes):
                result = (mixed[:, :LANES] / mixed[:, LANES:]).astype(jnp.bfloat16)
                for head in range(TOGETHER):
                    column = (at * TOGETHER + head) * LANES
                    result_ref[index, :, column : column + LANES] = result[head * cap : (head + 1) * cap]

        def body(index, carry):
            place, low = place_of(index), low_of(place_of(index))
            upper = place < blocks // 2
            lower = (place < blocks) & (place >= blocks // 2)
            variants = [
                (upper, 0, False, False),
                (lower & (low >= half), 1, False, False),
                (lower & (low < half), 1, True, False),
            ]
            if count == 1:
                variants = [(here & (low >= 0), *what) for here, *what in variants]
                variants += [(upper & (low < 0), 0, False, True), (lower & (low < 0), 1, True, True)]
            for here, *what in variants:
                pl.when(here)(functools.partial(one_block, index, place, *what))
            pl.when(place < blocks)(result_copy(index).start)
            return carry

        for index in range(parcels):

            @pl.when(place_of(index) < blocks)
            def _():
                stage_ref[index] = array_refs[0][index] if index < slots else array_refs[index - slots + (slots > 0)][...]

        lax.fori_loop(0, parcels, body, 0)
        for index in range(parcels):
            pl.when(place_of(index) < blocks)(result_copy(index).wait)

    operands = [meta, *own, *past, *arrays]
    specs = [SMEM] + [VMEM] * (len(operands) - 1)
    aliases = {}
    if out is not None:
        aliases = {len(operands): 0}
        operands.append(out)
        specs.append(ANY)
    area = max(1, parcels // 2) * heads * cap * (count + 1) * rows
    return pl.pallas_call(
        kernel,
        out_shape=jax.ShapeDtypeStruct((rows, width), jnp.bfloat16),
        in_specs=specs,
        out_specs=ANY,
        input_output_aliases=aliases,
        scratch_shapes=[
            pltpu.VMEM((parcels, cap, width), jnp.bfloat16),
            pltpu.VMEM((parcels, cap, width), jnp.bfloat16),
            pltpu.SemaphoreType.DMA((parcels,)),
        ],
        compiler_params=params(28),
        cost_estimate=pl.CostEstimate(
            flops=8 * area * LANES, bytes_accessed=4 * parcels * cap * width, transcendentals=area
        ),
        name="attend",
    )(*operands)


def digits(begin):
    lane = jnp.arange(LANES, dtype=jnp.int32)
    digit = jnp.where(lane < DIGIT, begin[..., None] // DIGIT, begin[..., None] % DIGIT)
    hit = digit == lane % DIGIT
    return jnp.where(hit, 1.0, 0.0).astype(jnp.bfloat16), jnp.where(hit, 0.0, -APART).astype(jnp.bfloat16)


def local(queries, keys_values, routing, documents):
    rows, width = queries.shape
    owners = lax.axis_size("dp")
    columns = lax.axis_size("ctx")
    kv_heads, pair, head_dim = keys_values.shape[1:]
    assert kv_heads == 1 and pair == 2 and head_dim == LANES
    cap = 2 * rows // owners
    blocks = rows // cap
    seq_len = rows * columns
    assert seq_len <= DIGIT * DIGIT
    half = owners // 2
    assert owners & (owners - 1) == 0
    column = lax.axis_index("ctx")
    me = lax.axis_index("dp")

    routing = routing.T
    send_kv = pack_kv(routing, documents.reshape(-1, LANES), keys_values.reshape(2 * rows, LANES), owners, seq_len)
    parcels = lax.all_to_all(send_kv, "dp", split_axis=0, concat_axis=0, tiled=True)
    near, *far = pack_q(routing, queries, send_kv, owners)
    groups = [list(range(half)), list(range(half, owners))]
    near = lax.all_to_all(near, "dp", split_axis=0, concat_axis=0, axis_index_groups=groups, tiled=True)
    label = parcels[:, :4].astype(jnp.float32).astype(jnp.int32)
    place, part = label[:, 2, 0], label[:, 3, 0]
    begin = (label[:, 0] * DIGIT + label[:, 1]).reshape(owners, LANES // cap, cap)
    slots = jnp.arange(blocks, dtype=jnp.int32)
    every = jnp.arange(owners, dtype=jnp.int32)
    chosen = place[None, :] == slots[:, None]
    source = jnp.sum(jnp.where(chosen, every[None, :], 0), axis=1)
    senders = jnp.concatenate([me // half * half + every[:half], me ^ jnp.roll(every[half:], 2)])
    places = jnp.sum(jnp.where(senders[:, None] == every[None, :], place[None, :], 0), axis=1)
    wanted = chosen[:, :, None] & (part[None, :, None] == jnp.arange(LANES // cap, dtype=jnp.int32))
    doc = jnp.sum(jnp.where(wanted[..., None], begin[None], 0), axis=(1, 2)).reshape(rows)

    split = jnp.concatenate([doc // DIGIT, doc % DIGIT]).astype(jnp.float32).astype(jnp.bfloat16).reshape(-1, LANES)
    split = jnp.pad(split, ((0, -split.shape[0] % LABEL_ROWS), (0, 0)))
    own_kv = place_kv(source, parcels, split, rows, cap)
    past_kv = lax.ppermute(own_kv, "ctx", [(0, 1)])[None] if columns == 2 else lax.all_gather(own_kv, "ctx")
    same, apart = digits(doc)
    own = (same, own_kv[: 2 * rows].reshape(rows, 2, LANES)[:, 0], apart, own_kv[: 2 * rows].reshape(rows, 2, LANES)[:, 1])
    past_doc = past_kv[:, 2 * rows :][:, : 2 * rows // LANES].reshape(-1, 2, rows).astype(jnp.float32).astype(jnp.int32)
    past_apart = digits(past_doc[:, 0] * DIGIT + past_doc[:, 1])[1]
    past_rows = past_kv[:, : 2 * rows].reshape(-1, rows, 2, LANES)
    past = (past_rows[:, :, 0], past_apart, past_rows[:, :, 1])

    lows = jnp.min(doc.reshape(blocks, cap), axis=1) - column * rows
    meta = jnp.concatenate([column[None], places, lows])
    sent, far = far, []
    for index, parcel in enumerate(sent):
        if index >= 4:
            ties = (past_kv,) if index >= half - 2 else (far[index - 4], own_kv)
            parcel = lax.optimization_barrier((parcel, *ties))[0]
        far.append(lax.ppermute(parcel, "dp", [(owner, owner ^ (half + index)) for owner in range(owners)]))
    out = attend(meta, half + 2, None, far[: half - 5], own, past, None)
    out = attend(meta, half + 2 + half - 5, None, far[half - 5 : half - 2], own, past, out)
    return attend(meta, 0, near, far[half - 2 :], own, past, out)


def solution(mesh):
    placed = (
        P(("dp", "ctx"), None),
        P(("dp", "ctx"), None, None, None),
        P(("dp", "ctx"), None),
        P(("dp", "ctx")),
    )
    return jax.shard_map(
        local, mesh=mesh, in_specs=placed, out_specs=P(("dp", "ctx"), None), check_vma=False
    )
```

```python
import functools
import math

import jax
import jax.numpy as jnp
from jax import lax
from jax.experimental import pallas as pl
from jax.experimental.pallas import tpu as pltpu
from jax.sharding import PartitionSpec as P

LANES = 128
LABEL_ROWS = 16
DIGIT = 64
TOGETHER = 4
APART = 16384.0
NEVER = -1e30
ANY = pl.BlockSpec(memory_space=pl.ANY)
VMEM = pl.BlockSpec(memory_space=pltpu.VMEM)
SMEM = pl.BlockSpec(memory_space=pltpu.SMEM)


def params(mib):
    return pltpu.CompilerParams(vmem_limit_bytes=mib * 1024 * 1024)


def hbm(*arrays):
    return [pltpu.with_memory_space_constraint(array, pltpu.HBM) for array in arrays]


def pack_kv(routing, documents, kv, owners, seq_len):
    rows = kv.shape[0] // 2
    cap = 2 * rows // owners
    blocks = rows // cap
    per_group = LANES // cap

    def kernel(routing_any, doc_any, kv_any, out_ref, routing_ref, doc_ref, kv_ref, label_ref, held_ref, in_sem, sem, label_sem):
        fetches = [
            pltpu.make_async_copy(source, target, in_sem.at[index])
            for index, (source, target) in enumerate(
                ((routing_any, routing_ref), (doc_any, doc_ref), (kv_any, kv_ref))
            )
        ]
        for fetch in fetches:
            fetch.start()
        fetches[0].wait()
        for slot in range(owners):
            held_ref[slot] = blocks
        for block in range(blocks):
            held_ref[routing_ref[0, block * cap]] = block
        fetches[1].wait()
        row_at = lax.broadcasted_iota(jnp.int32, (LABEL_ROWS, LANES), 0)
        label_ref[blocks] = jnp.full((LABEL_ROWS, LANES), 255.0, jnp.bfloat16)
        for block in range(blocks):
            group, part = divmod(block, per_group)
            begin = doc_ref[group : group + 1, :] - routing_ref[0, block * cap] * seq_len
            place = routing_ref[1, block * cap] // cap
            label = jnp.where(row_at == 0, begin // DIGIT, jnp.where(row_at == 1, begin % DIGIT, part))
            label = jnp.where(row_at == 2, place, label)
            label_ref[block] = label.astype(jnp.float32).astype(jnp.bfloat16)
        copies = [
            pltpu.make_async_copy(
                label_ref.at[held_ref[slot]], out_ref.at[slot, pl.ds(0, LABEL_ROWS)], label_sem.at[slot]
            )
            for slot in range(owners)
        ]
        for block in range(blocks):
            copies.append(
                pltpu.make_async_copy(
                    kv_ref.at[pl.ds(block * 2 * cap, 2 * cap)],
                    out_ref.at[routing_ref[0, block * cap], pl.ds(LABEL_ROWS, 2 * cap)],
                    sem.at[block],
                )
            )
        fetches[2].wait()
        for copy in copies:
            copy.start()
        for copy in copies:
            copy.wait()

    return pl.pallas_call(
        kernel,
        out_shape=pltpu.HBM((owners, LABEL_ROWS + 2 * cap, LANES), kv.dtype),
        in_specs=[ANY] * 3,
        out_specs=ANY,
        scratch_shapes=[
            pltpu.SMEM(routing.shape, jnp.int32),
            pltpu.VMEM(documents.shape, jnp.int32),
            pltpu.VMEM(kv.shape, kv.dtype),
            pltpu.VMEM((blocks + 1, LABEL_ROWS, LANES), jnp.bfloat16),
            pltpu.SMEM((owners,), jnp.int32),
            pltpu.SemaphoreType.DMA((3,)),
            pltpu.SemaphoreType.DMA((blocks,)),
            pltpu.SemaphoreType.DMA((owners,)),
        ],
        compiler_params=params(16),
        name="pack_kv",
    )(*hbm(routing, documents, kv))


def pack_q(routing, queries, earlier, owners):
    rows, width = queries.shape
    cap = 2 * rows // owners
    blocks = rows // cap
    half = owners // 2

    def kernel(routing_any, q_any, earlier_ref, near_ref, *rest):
        far_refs = rest[:half]
        routing_ref, q_ref, held_ref, in_sem, q_sem, sem = rest[half:]
        me = lax.axis_index("dp")
        fetch = pltpu.make_async_copy(routing_any, routing_ref, in_sem)
        fetch.start()
        fetch_q = pltpu.make_async_copy(q_any, q_ref, q_sem)
        fetch_q.start()
        fetch.wait()
        for slot in range(owners):
            held_ref[slot] = blocks
        for block in range(blocks):
            held_ref[routing_ref[0, block * cap]] = block
        copies = []
        for step in range(owners):
            slot = me ^ step
            block = held_ref[slot]
            q_rows = pl.ds(pl.multiple_of(jnp.minimum(block, blocks - 1) * cap, cap), cap)
            target = far_refs[step - half] if step >= half else near_ref.at[lax.rem(slot, half)]
            copies.append((block < blocks, pltpu.make_async_copy(q_ref.at[q_rows], target, sem.at[step])))
        fetch_q.wait()
        for held, copy in copies:
            pl.when(held)(copy.start)
        for held, copy in copies:
            pl.when(held)(copy.wait)

    return pl.pallas_call(
        kernel,
        out_shape=[
            pltpu.HBM((half, cap, width), queries.dtype),
            *[jax.ShapeDtypeStruct((cap, width), queries.dtype)] * half,
        ],
        in_specs=[ANY] * 3,
        out_specs=[ANY] * (1 + half),
        scratch_shapes=[
            pltpu.SMEM(routing.shape, jnp.int32),
            pltpu.VMEM(queries.shape, queries.dtype),
            pltpu.SMEM((owners,), jnp.int32),
            pltpu.SemaphoreType.DMA,
            pltpu.SemaphoreType.DMA,
            pltpu.SemaphoreType.DMA((owners,)),
        ],
        compiler_params=params(16),
        name="pack_q",
    )(*hbm(routing, queries, earlier))


def place_kv(source, parcels, begins, rows, cap):
    blocks = rows // cap

    def kernel(source_ref, in_ref, begin_ref, out_ref, sem):
        copies = [
            pltpu.make_async_copy(
                in_ref.at[source_ref[place], pl.ds(LABEL_ROWS, 2 * cap)],
                out_ref.at[pl.ds(place * 2 * cap, 2 * cap)],
                sem.at[place],
            )
            for place in range(blocks)
        ]
        copies.append(
            pltpu.make_async_copy(begin_ref, out_ref.at[pl.ds(2 * rows, begin_ref.shape[0])], sem.at[blocks])
        )
        for copy in copies:
            copy.start()
        for copy in copies:
            copy.wait()

    return pl.pallas_call(
        kernel,
        out_shape=jax.ShapeDtypeStruct((2 * rows + begins.shape[0], LANES), parcels.dtype),
        in_specs=[SMEM, ANY, ANY],
        out_specs=ANY,
        scratch_shapes=[pltpu.SemaphoreType.DMA((blocks + 1,))],
        compiler_params=params(16),
        name="place_kv",
    )(source, parcels, begins)


def attend(meta, first, near, far, own, past, out):
    rows = own[0].shape[0]
    cap, width = near.shape[1:] if far == [] else far[0].shape
    blocks = rows // cap
    heads = width // LANES
    half = rows // 2
    count = past[0].shape[0]
    slots = 0 if near is None else near.shape[0]
    parcels = slots + len(far)
    lows_at = meta.shape[0] - blocks
    factor = math.log2(math.e) / math.sqrt(LANES)
    arrays = ([] if near is None else [near]) + far

    def kernel(meta_ref, qd_ref, ok_ref, od_ref, ov_ref, pk_ref, pd_ref, pv_ref, *rest):
        array_refs = rest[: len(arrays)]
        out_any, stage_ref, result_ref, sem = rest[-4:]

        def keys(k_ref, d_ref):
            return jnp.concatenate([k_ref, d_ref], axis=1)

        def values(v):
            return jnp.concatenate([v, jnp.ones(v.shape, v.dtype)], axis=1)

        def scores(tile_q, tile_k):
            return lax.dot_general(tile_q, tile_k, (((1,), (1,)), ((), ())), preferred_element_type=jnp.float32)

        def top(raw):
            return jnp.max(raw, axis=-1, keepdims=True)

        def mix(raw, peak, tile_v):
            weights = jnp.exp2((raw - peak) * factor).astype(jnp.bfloat16)
            return jnp.dot(weights, tile_v, preferred_element_type=jnp.float32)

        def place_of(index):
            return meta_ref[1 + first + index]

        def low_of(place):
            return meta_ref[lows_at + jnp.minimum(place, blocks - 1)]

        def result_copy(index):
            at = pl.multiple_of(jnp.minimum(place_of(index), blocks - 1) * cap, cap)
            return pltpu.make_async_copy(result_ref.at[index], out_any.at[pl.ds(at, cap)], sem.at[index])

        def one_block(index, place, lower, with_low, with_past):
            block_q = stage_ref[index]
            same = qd_ref[pl.ds(pl.multiple_of(place * cap, cap), cap), :]
            same = jnp.concatenate([same] * TOGETHER, axis=0)
            row_at = lax.broadcasted_iota(jnp.int32, (cap, half), 0) + (place * cap - lower * half)
            seen = lax.broadcasted_iota(jnp.int32, (cap, half), 1) <= row_at
            last = pl.ds(lower * half, half)

            def causal(raw):
                return jnp.where(seen[None], raw.reshape(TOGETHER, cap, half), NEVER).reshape(TOGETHER * cap, half)

            tile_qs = []
            for begin in range(0, heads, TOGETHER):
                tiles = [block_q[:, head * LANES : (head + 1) * LANES] for head in range(begin, begin + TOGETHER)]
                tile_qs.append(jnp.concatenate([jnp.concatenate(tiles, axis=0), same], axis=1))
            raws = [[causal(scores(tile_q, keys(ok_ref[last], od_ref[last])))] for tile_q in tile_qs]
            tile_vs = [ov_ref[last]]
            if with_low:
                for several, tile_q in zip(raws, tile_qs):
                    several.append(scores(tile_q, keys(ok_ref[:half], od_ref[:half])))
                tile_vs.append(ov_ref[:half])
            if with_past:
                for several, tile_q in zip(raws, tile_qs):
                    several.append(scores(tile_q, keys(pk_ref[0], pd_ref[0])))
                tile_vs.append(pv_ref[0])
            peaks = [functools.reduce(jnp.maximum, [top(raw) for raw in several]) for several in raws]
            mixes = [
                sum(mix(raw, peak, values(tile_v)) for raw, tile_v in zip(several, tile_vs))
                for several, peak in zip(raws, peaks)
            ]
            if count > 1:

                def step(earlier, state):
                    result = []
                    for (peak, mixed), tile_q in zip(state, tile_qs):
                        raw = scores(tile_q, keys(pk_ref[earlier], pd_ref[earlier]))
                        higher = jnp.maximum(peak, top(raw))
                        decay = jnp.exp2((peak - higher) * factor)
                        result.append((higher, mixed * decay + mix(raw, higher, values(pv_ref[earlier]))))
                    return result

                least = jnp.maximum(low_of(place) + meta_ref[0] * rows, 0) // rows
                mixes = [mixed for _, mixed in lax.fori_loop(least, meta_ref[0], step, list(zip(peaks, mixes)))]
            for at, mixed in enumerate(mixes):
                result = (mixed[:, :LANES] / mixed[:, LANES:]).astype(jnp.bfloat16)
                for head in range(TOGETHER):
                    column = (at * TOGETHER + head) * LANES
                    result_ref[index, :, column : column + LANES] = result[head * cap : (head + 1) * cap]

        def body(index, carry):
            place, low = place_of(index), low_of(place_of(index))
            upper = place < blocks // 2
            lower = (place < blocks) & (place >= blocks // 2)
            variants = [
                (upper, 0, False, False),
                (lower & (low >= half), 1, False, False),
                (lower & (low < half), 1, True, False),
            ]
            if count == 1:
                variants = [(here & (low >= 0), *what) for here, *what in variants]
                variants += [(upper & (low < 0), 0, False, True), (lower & (low < 0), 1, True, True)]
            for here, *what in variants:
                pl.when(here)(functools.partial(one_block, index, place, *what))
            pl.when(place < blocks)(result_copy(index).start)
            return carry

        for index in range(parcels):

            @pl.when(place_of(index) < blocks)
            def _():
                stage_ref[index] = array_refs[0][index] if index < slots else array_refs[index - slots + (slots > 0)][...]

        lax.fori_loop(0, parcels, body, 0)
        for index in range(parcels):
            pl.when(place_of(index) < blocks)(result_copy(index).wait)

    operands = [meta, *own, *past, *arrays]
    specs = [SMEM] + [VMEM] * (len(operands) - 1)
    aliases = {}
    if out is not None:
        aliases = {len(operands): 0}
        operands.append(out)
        specs.append(ANY)
    area = max(1, parcels // 2) * heads * cap * (count + 1) * rows
    return pl.pallas_call(
        kernel,
        out_shape=jax.ShapeDtypeStruct((rows, width), jnp.bfloat16),
        in_specs=specs,
        out_specs=ANY,
        input_output_aliases=aliases,
        scratch_shapes=[
            pltpu.VMEM((parcels, cap, width), jnp.bfloat16),
            pltpu.VMEM((parcels, cap, width), jnp.bfloat16),
            pltpu.SemaphoreType.DMA((parcels,)),
        ],
        compiler_params=params(28),
        cost_estimate=pl.CostEstimate(
            flops=8 * area * LANES, bytes_accessed=4 * parcels * cap * width, transcendentals=area
        ),
        name="attend",
    )(*operands)


def digits(begin):
    lane = jnp.arange(LANES, dtype=jnp.int32)
    digit = jnp.where(lane < DIGIT, begin[..., None] // DIGIT, begin[..., None] % DIGIT)
    hit = digit == lane % DIGIT
    return jnp.where(hit, 1.0, 0.0).astype(jnp.bfloat16), jnp.where(hit, 0.0, -APART).astype(jnp.bfloat16)


def local(queries, keys_values, routing, documents):
    rows, width = queries.shape
    owners = lax.axis_size("dp")
    columns = lax.axis_size("ctx")
    kv_heads, pair, head_dim = keys_values.shape[1:]
    assert kv_heads == 1 and pair == 2 and head_dim == LANES
    cap = 2 * rows // owners
    blocks = rows // cap
    seq_len = rows * columns
    assert seq_len <= DIGIT * DIGIT
    half = owners // 2
    assert owners & (owners - 1) == 0
    column = lax.axis_index("ctx")
    me = lax.axis_index("dp")

    routing = routing.T
    send_kv = pack_kv(routing, documents.reshape(-1, LANES), keys_values.reshape(2 * rows, LANES), owners, seq_len)
    parcels = lax.all_to_all(send_kv, "dp", split_axis=0, concat_axis=0, tiled=True)
    near, *far = pack_q(routing, queries, send_kv, owners)
    groups = [list(range(half)), list(range(half, owners))]
    near = lax.all_to_all(near, "dp", split_axis=0, concat_axis=0, axis_index_groups=groups, tiled=True)
    label = parcels[:, :4].astype(jnp.float32).astype(jnp.int32)
    place, part = label[:, 2, 0], label[:, 3, 0]
    begin = (label[:, 0] * DIGIT + label[:, 1]).reshape(owners, LANES // cap, cap)
    slots = jnp.arange(blocks, dtype=jnp.int32)
    every = jnp.arange(owners, dtype=jnp.int32)
    chosen = place[None, :] == slots[:, None]
    source = jnp.sum(jnp.where(chosen, every[None, :], 0), axis=1)
    senders = jnp.concatenate([me // half * half + every[:half], me ^ every[half:]])
    places = jnp.sum(jnp.where(senders[:, None] == every[None, :], place[None, :], 0), axis=1)
    wanted = chosen[:, :, None] & (part[None, :, None] == jnp.arange(LANES // cap, dtype=jnp.int32))
    doc = jnp.sum(jnp.where(wanted[..., None], begin[None], 0), axis=(1, 2)).reshape(rows)

    split = jnp.concatenate([doc // DIGIT, doc % DIGIT]).astype(jnp.float32).astype(jnp.bfloat16).reshape(-1, LANES)
    split = jnp.pad(split, ((0, -split.shape[0] % LABEL_ROWS), (0, 0)))
    own_kv = place_kv(source, parcels, split, rows, cap)
    past_kv = lax.ppermute(own_kv, "ctx", [(0, 1)])[None] if columns == 2 else lax.all_gather(own_kv, "ctx")
    same, apart = digits(doc)
    own = (same, own_kv[: 2 * rows].reshape(rows, 2, LANES)[:, 0], apart, own_kv[: 2 * rows].reshape(rows, 2, LANES)[:, 1])
    past_doc = past_kv[:, 2 * rows :][:, : 2 * rows // LANES].reshape(-1, 2, rows).astype(jnp.float32).astype(jnp.int32)
    past_apart = digits(past_doc[:, 0] * DIGIT + past_doc[:, 1])[1]
    past_rows = past_kv[:, : 2 * rows].reshape(-1, rows, 2, LANES)
    past = (past_rows[:, :, 0], past_apart, past_rows[:, :, 1])

    lows = jnp.min(doc.reshape(blocks, cap), axis=1) - column * rows
    meta = jnp.concatenate([column[None], places, lows])
    sent, far = far, []
    for index, parcel in enumerate(sent):
        if index >= 4:
            ties = (past_kv,) if index >= half - 2 else (far[index - 4], own_kv)
            parcel = lax.optimization_barrier((parcel, *ties))[0]
        far.append(lax.ppermute(parcel, "dp", [(owner, owner ^ (half + index)) for owner in range(owners)]))
    out = attend(meta, half, None, far[: half - 5], own, past, None)
    out = attend(meta, half + half - 5, None, far[half - 5 : half - 2], own, past, out)
    out = attend(meta, 0, near, [], own, past, out)
    return attend(meta, half + half - 2, None, far[half - 2 :], own, past, out)


def solution(mesh):
    placed = (
        P(("dp", "ctx"), None),
        P(("dp", "ctx"), None, None, None),
        P(("dp", "ctx"), None),
        P(("dp", "ctx")),
    )
    return jax.shard_map(
        local, mesh=mesh, in_specs=placed, out_specs=P(("dp", "ctx"), None), check_vma=False
    )
```

```python
import functools
import math

import jax
import jax.numpy as jnp
from jax import lax
from jax.experimental import pallas as pl
from jax.experimental.pallas import tpu as pltpu
from jax.sharding import PartitionSpec as P

LANES = 128
LABEL_ROWS = 16
DIGIT = 64
TOGETHER = 4
APART = 16384.0
NEVER = -1e30
ANY = pl.BlockSpec(memory_space=pl.ANY)
VMEM = pl.BlockSpec(memory_space=pltpu.VMEM)
SMEM = pl.BlockSpec(memory_space=pltpu.SMEM)


def params(mib):
    return pltpu.CompilerParams(vmem_limit_bytes=mib * 1024 * 1024)


def hbm(*arrays):
    return [pltpu.with_memory_space_constraint(array, pltpu.HBM) for array in arrays]


def pack_kv(routing, documents, kv, owners, seq_len):
    rows = kv.shape[0] // 2
    cap = 2 * rows // owners
    blocks = rows // cap
    per_group = LANES // cap

    def kernel(routing_any, doc_any, kv_any, out_ref, routing_ref, doc_ref, kv_ref, label_ref, held_ref, in_sem, sem, label_sem):
        fetches = [
            pltpu.make_async_copy(source, target, in_sem.at[index])
            for index, (source, target) in enumerate(
                ((routing_any, routing_ref), (doc_any, doc_ref), (kv_any, kv_ref))
            )
        ]
        for fetch in fetches:
            fetch.start()
        fetches[0].wait()
        for slot in range(owners):
            held_ref[slot] = blocks
        for block in range(blocks):
            held_ref[routing_ref[0, block * cap]] = block
        fetches[1].wait()
        row_at = lax.broadcasted_iota(jnp.int32, (LABEL_ROWS, LANES), 0)
        label_ref[blocks] = jnp.full((LABEL_ROWS, LANES), 255.0, jnp.bfloat16)
        for block in range(blocks):
            group, part = divmod(block, per_group)
            begin = doc_ref[group : group + 1, :] - routing_ref[0, block * cap] * seq_len
            place = routing_ref[1, block * cap] // cap
            label = jnp.where(row_at == 0, begin // DIGIT, jnp.where(row_at == 1, begin % DIGIT, part))
            label = jnp.where(row_at == 2, place, label)
            label_ref[block] = label.astype(jnp.float32).astype(jnp.bfloat16)
        copies = [
            pltpu.make_async_copy(
                label_ref.at[held_ref[slot]], out_ref.at[slot, pl.ds(0, LABEL_ROWS)], label_sem.at[slot]
            )
            for slot in range(owners)
        ]
        for block in range(blocks):
            copies.append(
                pltpu.make_async_copy(
                    kv_ref.at[pl.ds(block * 2 * cap, 2 * cap)],
                    out_ref.at[routing_ref[0, block * cap], pl.ds(LABEL_ROWS, 2 * cap)],
                    sem.at[block],
                )
            )
        fetches[2].wait()
        for copy in copies:
            copy.start()
        for copy in copies:
            copy.wait()

    return pl.pallas_call(
        kernel,
        out_shape=pltpu.HBM((owners, LABEL_ROWS + 2 * cap, LANES), kv.dtype),
        in_specs=[ANY] * 3,
        out_specs=ANY,
        scratch_shapes=[
            pltpu.SMEM(routing.shape, jnp.int32),
            pltpu.VMEM(documents.shape, jnp.int32),
            pltpu.VMEM(kv.shape, kv.dtype),
            pltpu.VMEM((blocks + 1, LABEL_ROWS, LANES), jnp.bfloat16),
            pltpu.SMEM((owners,), jnp.int32),
            pltpu.SemaphoreType.DMA((3,)),
            pltpu.SemaphoreType.DMA((blocks,)),
            pltpu.SemaphoreType.DMA((owners,)),
        ],
        compiler_params=params(16),
        name="pack_kv",
    )(*hbm(routing, documents, kv))


def pack_q(routing, queries, earlier, owners):
    rows, width = queries.shape
    cap = 2 * rows // owners
    blocks = rows // cap
    half = owners // 2

    def kernel(routing_any, q_any, earlier_ref, near_ref, *rest):
        far_refs = rest[:half]
        routing_ref, q_ref, held_ref, in_sem, q_sem, sem = rest[half:]
        me = lax.axis_index("dp")
        fetch = pltpu.make_async_copy(routing_any, routing_ref, in_sem)
        fetch.start()
        fetch_q = pltpu.make_async_copy(q_any, q_ref, q_sem)
        fetch_q.start()
        fetch.wait()
        for slot in range(owners):
            held_ref[slot] = blocks
        for block in range(blocks):
            held_ref[routing_ref[0, block * cap]] = block
        copies = []
        for step in range(owners):
            slot = me ^ step
            block = held_ref[slot]
            q_rows = pl.ds(pl.multiple_of(jnp.minimum(block, blocks - 1) * cap, cap), cap)
            target = far_refs[step - half] if step >= half else near_ref.at[lax.rem(slot, half)]
            copies.append((block < blocks, pltpu.make_async_copy(q_ref.at[q_rows], target, sem.at[step])))
        fetch_q.wait()
        for held, copy in copies:
            pl.when(held)(copy.start)
        for held, copy in copies:
            pl.when(held)(copy.wait)

    return pl.pallas_call(
        kernel,
        out_shape=[
            pltpu.HBM((half, cap, width), queries.dtype),
            *[jax.ShapeDtypeStruct((cap, width), queries.dtype)] * half,
        ],
        in_specs=[ANY] * 3,
        out_specs=[ANY] * (1 + half),
        scratch_shapes=[
            pltpu.SMEM(routing.shape, jnp.int32),
            pltpu.VMEM(queries.shape, queries.dtype),
            pltpu.SMEM((owners,), jnp.int32),
            pltpu.SemaphoreType.DMA,
            pltpu.SemaphoreType.DMA,
            pltpu.SemaphoreType.DMA((owners,)),
        ],
        compiler_params=params(16),
        name="pack_q",
    )(*hbm(routing, queries, earlier))


def place_kv(source, parcels, begins, rows, cap):
    blocks = rows // cap

    def kernel(source_ref, in_ref, begin_ref, out_ref, sem):
        copies = [
            pltpu.make_async_copy(
                in_ref.at[source_ref[place], pl.ds(LABEL_ROWS, 2 * cap)],
                out_ref.at[pl.ds(place * 2 * cap, 2 * cap)],
                sem.at[place],
            )
            for place in range(blocks)
        ]
        copies.append(
            pltpu.make_async_copy(begin_ref, out_ref.at[pl.ds(2 * rows, begin_ref.shape[0])], sem.at[blocks])
        )
        for copy in copies:
            copy.start()
        for copy in copies:
            copy.wait()

    return pl.pallas_call(
        kernel,
        out_shape=jax.ShapeDtypeStruct((2 * rows + begins.shape[0], LANES), parcels.dtype),
        in_specs=[SMEM, ANY, ANY],
        out_specs=ANY,
        scratch_shapes=[pltpu.SemaphoreType.DMA((blocks + 1,))],
        compiler_params=params(16),
        name="place_kv",
    )(source, parcels, begins)


def attend(meta, first, near, far, own, past, out):
    rows = own[0].shape[0]
    cap, width = near.shape[1:] if far == [] else far[0].shape
    blocks = rows // cap
    heads = width // LANES
    half = rows // 2
    count = past[0].shape[0]
    slots = 0 if near is None else near.shape[0]
    parcels = slots + len(far)
    lows_at = meta.shape[0] - blocks
    factor = math.log2(math.e) / math.sqrt(LANES)
    arrays = ([] if near is None else [near]) + far

    def kernel(meta_ref, qd_ref, ok_ref, od_ref, ov_ref, pk_ref, pd_ref, pv_ref, *rest):
        array_refs = rest[: len(arrays)]
        out_any, stage_ref, result_ref, list_ref, sem = rest[-5:]

        def keys(k_ref, d_ref):
            return jnp.concatenate([k_ref, d_ref], axis=1)

        def values(v):
            return jnp.concatenate([v, jnp.ones(v.shape, v.dtype)], axis=1)

        def scores(tile_q, tile_k):
            return lax.dot_general(tile_q, tile_k, (((1,), (1,)), ((), ())), preferred_element_type=jnp.float32)

        def top(raw):
            return jnp.max(raw, axis=-1, keepdims=True)

        def mix(raw, peak, tile_v):
            weights = jnp.exp2((raw - peak) * factor).astype(jnp.bfloat16)
            return jnp.dot(weights, tile_v, preferred_element_type=jnp.float32)

        def place_of(index):
            return meta_ref[1 + first + index]

        def low_of(place):
            return meta_ref[lows_at + jnp.minimum(place, blocks - 1)]

        def result_copy(index):
            at = pl.multiple_of(jnp.minimum(place_of(index), blocks - 1) * cap, cap)
            return pltpu.make_async_copy(result_ref.at[index], out_any.at[pl.ds(at, cap)], sem.at[index])

        def some_blocks(indices, places, seen_keys, with_past):
            tile_qs, raws = [], []
            for index, place in zip(indices, places):
                block_q = stage_ref[index]
                same = qd_ref[pl.ds(pl.multiple_of(place * cap, cap), cap), :]
                same = jnp.concatenate([same] * TOGETHER, axis=0)
                row_at = lax.broadcasted_iota(jnp.int32, (cap, seen_keys), 0) + place * cap
                seen = lax.broadcasted_iota(jnp.int32, (cap, seen_keys), 1) <= row_at
                for begin in range(0, heads, TOGETHER):
                    tiles = [block_q[:, head * LANES : (head + 1) * LANES] for head in range(begin, begin + TOGETHER)]
                    tile_q = jnp.concatenate([jnp.concatenate(tiles, axis=0), same], axis=1)
                    raw = scores(tile_q, keys(ok_ref[:seen_keys], od_ref[:seen_keys]))
                    raw = jnp.where(seen[None], raw.reshape(TOGETHER, cap, seen_keys), NEVER)
                    tile_qs.append(tile_q)
                    raws.append([raw.reshape(TOGETHER * cap, seen_keys)])
            tile_vs = [ov_ref[:seen_keys]]
            if with_past:
                for several, tile_q in zip(raws, tile_qs):
                    several.append(scores(tile_q, keys(pk_ref[0], pd_ref[0])))
                tile_vs.append(pv_ref[0])
            peaks = [functools.reduce(jnp.maximum, [top(raw) for raw in several]) for several in raws]
            mixes = [
                sum(mix(raw, peak, values(tile_v)) for raw, tile_v in zip(several, tile_vs))
                for several, peak in zip(raws, peaks)
            ]
            if count > 1:

                def step(earlier, state):
                    result = []
                    for (peak, mixed), tile_q in zip(state, tile_qs):
                        raw = scores(tile_q, keys(pk_ref[earlier], pd_ref[earlier]))
                        higher = jnp.maximum(peak, top(raw))
                        decay = jnp.exp2((peak - higher) * factor)
                        result.append((higher, mixed * decay + mix(raw, higher, values(pv_ref[earlier]))))
                    return result

                low = functools.reduce(jnp.minimum, [low_of(place) for place in places])
                least = jnp.maximum(low + meta_ref[0] * rows, 0) // rows
                mixes = [mixed for _, mixed in lax.fori_loop(least, meta_ref[0], step, list(zip(peaks, mixes)))]
            groups = heads // TOGETHER
            for at, mixed in enumerate(mixes):
                result = (mixed[:, :LANES] / mixed[:, LANES:]).astype(jnp.bfloat16)
                for head in range(TOGETHER):
                    column = (at % groups * TOGETHER + head) * LANES
                    result_ref[indices[at // groups], :, column : column + LANES] = result[head * cap : (head + 1) * cap]

        def body(pair, carry):
            indices = [list_ref[2 * pair], list_ref[2 * pair + 1]]
            places = [place_of(index) for index in indices]
            low = jnp.minimum(*[low_of(place) for place in places])
            short = jnp.maximum(*places) < blocks // 2
            for seen_keys, here in ((half, short), (rows, jnp.logical_not(short))):
                if count > 1:
                    pl.when(here)(functools.partial(some_blocks, indices, places, seen_keys, False))
                else:
                    pl.when(here & (low >= 0))(functools.partial(some_blocks, indices, places, seen_keys, False))
                    pl.when(here & (low < 0))(functools.partial(some_blocks, indices, places, seen_keys, True))
            result_copy(indices[0]).start()
            pl.when(indices[0] != indices[1])(result_copy(indices[1]).start)
            return carry

        held = jnp.int32(0)
        for index in range(parcels):
            list_ref[held] = index
            held += jnp.where(place_of(index) < blocks, 1, 0)
        list_ref[held] = list_ref[jnp.maximum(held - 1, 0)]

        for index in range(parcels):

            @pl.when(place_of(index) < blocks)
            def _():
                stage_ref[index] = array_refs[0][index] if index < slots else array_refs[index - slots + (slots > 0)][...]

        lax.fori_loop(0, (held + 1) // 2, body, 0)
        for index in range(parcels):
            pl.when(place_of(index) < blocks)(result_copy(index).wait)

    operands = [meta, *own, *past, *arrays]
    specs = [SMEM] + [VMEM] * (len(operands) - 1)
    aliases = {}
    if out is not None:
        aliases = {len(operands): 0}
        operands.append(out)
        specs.append(ANY)
    area = max(1, parcels // 2) * heads * cap * (count + 1) * rows
    return pl.pallas_call(
        kernel,
        out_shape=jax.ShapeDtypeStruct((rows, width), jnp.bfloat16),
        in_specs=specs,
        out_specs=ANY,
        input_output_aliases=aliases,
        scratch_shapes=[
            pltpu.VMEM((parcels, cap, width), jnp.bfloat16),
            pltpu.VMEM((parcels, cap, width), jnp.bfloat16),
            pltpu.SMEM((parcels + 1,), jnp.int32),
            pltpu.SemaphoreType.DMA((parcels,)),
        ],
        compiler_params=params(28),
        cost_estimate=pl.CostEstimate(
            flops=8 * area * LANES, bytes_accessed=4 * parcels * cap * width, transcendentals=area
        ),
        name="attend",
    )(*operands)


def digits(begin):
    lane = jnp.arange(LANES, dtype=jnp.int32)
    digit = jnp.where(lane < DIGIT, begin[..., None] // DIGIT, begin[..., None] % DIGIT)
    hit = digit == lane % DIGIT
    return jnp.where(hit, 1.0, 0.0).astype(jnp.bfloat16), jnp.where(hit, 0.0, -APART).astype(jnp.bfloat16)


def local(queries, keys_values, routing, documents):
    rows, width = queries.shape
    owners = lax.axis_size("dp")
    columns = lax.axis_size("ctx")
    kv_heads, pair, head_dim = keys_values.shape[1:]
    assert kv_heads == 1 and pair == 2 and head_dim == LANES
    cap = 2 * rows // owners
    blocks = rows // cap
    seq_len = rows * columns
    assert seq_len <= DIGIT * DIGIT
    half = owners // 2
    assert owners & (owners - 1) == 0
    column = lax.axis_index("ctx")
    me = lax.axis_index("dp")

    routing = routing.T
    send_kv = pack_kv(routing, documents.reshape(-1, LANES), keys_values.reshape(2 * rows, LANES), owners, seq_len)
    parcels = lax.all_to_all(send_kv, "dp", split_axis=0, concat_axis=0, tiled=True)
    near, *far = pack_q(routing, queries, send_kv, owners)
    groups = [list(range(half)), list(range(half, owners))]
    near = lax.all_to_all(near, "dp", split_axis=0, concat_axis=0, axis_index_groups=groups, tiled=True)
    label = parcels[:, :4].astype(jnp.float32).astype(jnp.int32)
    place, part = label[:, 2, 0], label[:, 3, 0]
    begin = (label[:, 0] * DIGIT + label[:, 1]).reshape(owners, LANES // cap, cap)
    slots = jnp.arange(blocks, dtype=jnp.int32)
    every = jnp.arange(owners, dtype=jnp.int32)
    chosen = place[None, :] == slots[:, None]
    source = jnp.sum(jnp.where(chosen, every[None, :], 0), axis=1)
    senders = jnp.concatenate([me // half * half + every[:half], me ^ every[half:]])
    places = jnp.sum(jnp.where(senders[:, None] == every[None, :], place[None, :], 0), axis=1)
    wanted = chosen[:, :, None] & (part[None, :, None] == jnp.arange(LANES // cap, dtype=jnp.int32))
    doc = jnp.sum(jnp.where(wanted[..., None], begin[None], 0), axis=(1, 2)).reshape(rows)

    split = jnp.concatenate([doc // DIGIT, doc % DIGIT]).astype(jnp.float32).astype(jnp.bfloat16).reshape(-1, LANES)
    split = jnp.pad(split, ((0, -split.shape[0] % LABEL_ROWS), (0, 0)))
    own_kv = place_kv(source, parcels, split, rows, cap)
    past_kv = lax.ppermute(own_kv, "ctx", [(0, 1)])[None] if columns == 2 else lax.all_gather(own_kv, "ctx")
    same, apart = digits(doc)
    own = (same, own_kv[: 2 * rows].reshape(rows, 2, LANES)[:, 0], apart, own_kv[: 2 * rows].reshape(rows, 2, LANES)[:, 1])
    past_doc = past_kv[:, 2 * rows :][:, : 2 * rows // LANES].reshape(-1, 2, rows).astype(jnp.float32).astype(jnp.int32)
    past_apart = digits(past_doc[:, 0] * DIGIT + past_doc[:, 1])[1]
    past_rows = past_kv[:, : 2 * rows].reshape(-1, rows, 2, LANES)
    past = (past_rows[:, :, 0], past_apart, past_rows[:, :, 1])

    lows = jnp.min(doc.reshape(blocks, cap), axis=1) - column * rows
    meta = jnp.concatenate([column[None], places, lows])
    sent, far = far, []
    for index, parcel in enumerate(sent):
        if index >= 4:
            ties = (past_kv,) if index >= half - 2 else (far[index - 4], own_kv)
            parcel = lax.optimization_barrier((parcel, *ties))[0]
        far.append(lax.ppermute(parcel, "dp", [(owner, owner ^ (half + index)) for owner in range(owners)]))
    out = attend(meta, half, None, far[: half - 5], own, past, None)
    out = attend(meta, half + half - 5, None, far[half - 5 : half - 2], own, past, out)
    out = attend(meta, 0, near, [], own, past, out)
    return attend(meta, half + half - 2, None, far[half - 2 :], own, past, out)


def solution(mesh):
    placed = (
        P(("dp", "ctx"), None),
        P(("dp", "ctx"), None, None, None),
        P(("dp", "ctx"), None),
        P(("dp", "ctx")),
    )
    return jax.shard_map(
        local, mesh=mesh, in_specs=placed, out_specs=P(("dp", "ctx"), None), check_vma=False
    )
```

```python
import functools
import math

import jax
import jax.numpy as jnp
from jax import lax
from jax.experimental import pallas as pl
from jax.experimental.pallas import tpu as pltpu
from jax.sharding import PartitionSpec as P

LANES = 128
LABEL_ROWS = 16
DIGIT = 64
TOGETHER = 4
APART = 16384.0
NEVER = -1e30
ANY = pl.BlockSpec(memory_space=pl.ANY)
VMEM = pl.BlockSpec(memory_space=pltpu.VMEM)
SMEM = pl.BlockSpec(memory_space=pltpu.SMEM)


def params(mib):
    return pltpu.CompilerParams(vmem_limit_bytes=mib * 1024 * 1024)


def hbm(*arrays):
    return [pltpu.with_memory_space_constraint(array, pltpu.HBM) for array in arrays]


def pack_kv(routing, documents, kv, owners, seq_len):
    rows = kv.shape[0] // 2
    cap = 2 * rows // owners
    blocks = rows // cap
    per_group = LANES // cap

    def kernel(routing_any, doc_any, kv_any, out_ref, routing_ref, doc_ref, kv_ref, label_ref, held_ref, in_sem, sem, label_sem):
        fetches = [
            pltpu.make_async_copy(source, target, in_sem.at[index])
            for index, (source, target) in enumerate(
                ((routing_any, routing_ref), (doc_any, doc_ref), (kv_any, kv_ref))
            )
        ]
        for fetch in fetches:
            fetch.start()
        fetches[0].wait()
        for slot in range(owners):
            held_ref[slot] = blocks
        for block in range(blocks):
            held_ref[routing_ref[0, block * cap]] = block
        fetches[1].wait()
        row_at = lax.broadcasted_iota(jnp.int32, (LABEL_ROWS, LANES), 0)
        label_ref[blocks] = jnp.full((LABEL_ROWS, LANES), 255.0, jnp.bfloat16)
        for block in range(blocks):
            group, part = divmod(block, per_group)
            begin = doc_ref[group : group + 1, :] - routing_ref[0, block * cap] * seq_len
            place = routing_ref[1, block * cap] // cap
            label = jnp.where(row_at == 0, begin // DIGIT, jnp.where(row_at == 1, begin % DIGIT, part))
            label = jnp.where(row_at == 2, place, label)
            label_ref[block] = label.astype(jnp.float32).astype(jnp.bfloat16)
        copies = [
            pltpu.make_async_copy(
                label_ref.at[held_ref[slot]], out_ref.at[slot, pl.ds(0, LABEL_ROWS)], label_sem.at[slot]
            )
            for slot in range(owners)
        ]
        for block in range(blocks):
            copies.append(
                pltpu.make_async_copy(
                    kv_ref.at[pl.ds(block * 2 * cap, 2 * cap)],
                    out_ref.at[routing_ref[0, block * cap], pl.ds(LABEL_ROWS, 2 * cap)],
                    sem.at[block],
                )
            )
        fetches[2].wait()
        for copy in copies:
            copy.start()
        for copy in copies:
            copy.wait()

    return pl.pallas_call(
        kernel,
        out_shape=pltpu.HBM((owners, LABEL_ROWS + 2 * cap, LANES), kv.dtype),
        in_specs=[ANY] * 3,
        out_specs=ANY,
        scratch_shapes=[
            pltpu.SMEM(routing.shape, jnp.int32),
            pltpu.VMEM(documents.shape, jnp.int32),
            pltpu.VMEM(kv.shape, kv.dtype),
            pltpu.VMEM((blocks + 1, LABEL_ROWS, LANES), jnp.bfloat16),
            pltpu.SMEM((owners,), jnp.int32),
            pltpu.SemaphoreType.DMA((3,)),
            pltpu.SemaphoreType.DMA((blocks,)),
            pltpu.SemaphoreType.DMA((owners,)),
        ],
        compiler_params=params(16),
        name="pack_kv",
    )(*hbm(routing, documents, kv))


def pack_q(routing, queries, earlier, owners):
    rows, width = queries.shape
    cap = 2 * rows // owners
    blocks = rows // cap
    half = owners // 2

    def kernel(routing_any, q_any, earlier_ref, near_ref, *rest):
        far_refs = rest[:half]
        routing_ref, q_ref, held_ref, in_sem, q_sem, sem = rest[half:]
        me = lax.axis_index("dp")
        fetch = pltpu.make_async_copy(routing_any, routing_ref, in_sem)
        fetch.start()
        fetch_q = pltpu.make_async_copy(q_any, q_ref, q_sem)
        fetch_q.start()
        fetch.wait()
        for slot in range(owners):
            held_ref[slot] = blocks
        for block in range(blocks):
            held_ref[routing_ref[0, block * cap]] = block
        copies = []
        for step in range(owners):
            slot = me ^ step
            block = held_ref[slot]
            q_rows = pl.ds(pl.multiple_of(jnp.minimum(block, blocks - 1) * cap, cap), cap)
            target = far_refs[step - half] if step >= half else near_ref.at[lax.rem(slot, half)]
            copies.append((block < blocks, pltpu.make_async_copy(q_ref.at[q_rows], target, sem.at[step])))
        fetch_q.wait()
        for held, copy in copies:
            pl.when(held)(copy.start)
        for held, copy in copies:
            pl.when(held)(copy.wait)

    return pl.pallas_call(
        kernel,
        out_shape=[
            pltpu.HBM((half, cap, width), queries.dtype),
            *[jax.ShapeDtypeStruct((cap, width), queries.dtype)] * half,
        ],
        in_specs=[ANY] * 3,
        out_specs=[ANY] * (1 + half),
        scratch_shapes=[
            pltpu.SMEM(routing.shape, jnp.int32),
            pltpu.VMEM(queries.shape, queries.dtype),
            pltpu.SMEM((owners,), jnp.int32),
            pltpu.SemaphoreType.DMA,
            pltpu.SemaphoreType.DMA,
            pltpu.SemaphoreType.DMA((owners,)),
        ],
        compiler_params=params(16),
        name="pack_q",
    )(*hbm(routing, queries, earlier))


def place_kv(source, parcels, begins, rows, cap):
    blocks = rows // cap

    def kernel(source_ref, in_ref, begin_ref, out_ref, sem):
        copies = [
            pltpu.make_async_copy(
                in_ref.at[source_ref[place], pl.ds(LABEL_ROWS, 2 * cap)],
                out_ref.at[pl.ds(place * 2 * cap, 2 * cap)],
                sem.at[place],
            )
            for place in range(blocks)
        ]
        copies.append(
            pltpu.make_async_copy(begin_ref, out_ref.at[pl.ds(2 * rows, begin_ref.shape[0])], sem.at[blocks])
        )
        for copy in copies:
            copy.start()
        for copy in copies:
            copy.wait()

    return pl.pallas_call(
        kernel,
        out_shape=jax.ShapeDtypeStruct((2 * rows + begins.shape[0], LANES), parcels.dtype),
        in_specs=[SMEM, ANY, ANY],
        out_specs=ANY,
        scratch_shapes=[pltpu.SemaphoreType.DMA((blocks + 1,))],
        compiler_params=params(16),
        name="place_kv",
    )(source, parcels, begins)


def attend(meta, first, near, far, own, past, out):
    rows = own[0].shape[0]
    cap, width = near.shape[1:] if far == [] else far[0].shape
    blocks = rows // cap
    heads = width // LANES
    half = rows // 2
    count = past[0].shape[0]
    slots = 0 if near is None else near.shape[0]
    parcels = slots + len(far)
    lows_at = meta.shape[0] - blocks
    factor = math.log2(math.e) / math.sqrt(LANES)
    arrays = ([] if near is None else [near]) + far

    def kernel(meta_ref, qd_ref, ok_ref, od_ref, ov_ref, pk_ref, pd_ref, pv_ref, *rest):
        array_refs = rest[: len(arrays)]
        out_any, stage_ref, result_ref, list_ref, sem = rest[-5:]

        def keys(k_ref, d_ref):
            return jnp.concatenate([k_ref, d_ref], axis=1)

        def values(v):
            return jnp.concatenate([v, jnp.ones(v.shape, v.dtype)], axis=1)

        def scores(tile_q, tile_k):
            return lax.dot_general(tile_q, tile_k, (((1,), (1,)), ((), ())), preferred_element_type=jnp.float32)

        def top(raw):
            return jnp.max(raw, axis=-1, keepdims=True)

        def mix(raw, peak, tile_v):
            weights = jnp.exp2((raw - peak) * factor).astype(jnp.bfloat16)
            return jnp.dot(weights, tile_v, preferred_element_type=jnp.float32)

        def place_of(index):
            return meta_ref[1 + first + index]

        def low_of(place):
            return meta_ref[lows_at + jnp.minimum(place, blocks - 1)]

        def result_copy(index):
            at = pl.multiple_of(jnp.minimum(place_of(index), blocks - 1) * cap, cap)
            return pltpu.make_async_copy(result_ref.at[index], out_any.at[pl.ds(at, cap)], sem.at[index])

        def some_blocks(indices, places, seen_keys, with_past):
            tile_qs, raws = [], []
            for index, place in zip(indices, places):
                block_q = stage_ref[index]
                same = qd_ref[pl.ds(pl.multiple_of(place * cap, cap), cap), :]
                same = jnp.concatenate([same] * TOGETHER, axis=0)
                row_at = lax.broadcasted_iota(jnp.int32, (cap, seen_keys), 0) + place * cap
                seen = lax.broadcasted_iota(jnp.int32, (cap, seen_keys), 1) <= row_at
                for begin in range(0, heads, TOGETHER):
                    tiles = [block_q[:, head * LANES : (head + 1) * LANES] for head in range(begin, begin + TOGETHER)]
                    tile_q = jnp.concatenate([jnp.concatenate(tiles, axis=0), same], axis=1)
                    raw = scores(tile_q, keys(ok_ref[:seen_keys], od_ref[:seen_keys]))
                    raw = jnp.where(seen[None], raw.reshape(TOGETHER, cap, seen_keys), NEVER)
                    tile_qs.append(tile_q)
                    raws.append([raw.reshape(TOGETHER * cap, seen_keys)])
            tile_vs = [ov_ref[:seen_keys]]
            if with_past:
                for several, tile_q in zip(raws, tile_qs):
                    several.append(scores(tile_q, keys(pk_ref[0], pd_ref[0])))
                tile_vs.append(pv_ref[0])
            peaks = [functools.reduce(jnp.maximum, [top(raw) for raw in several]) for several in raws]
            mixes = [
                sum(mix(raw, peak, values(tile_v)) for raw, tile_v in zip(several, tile_vs))
                for several, peak in zip(raws, peaks)
            ]
            if count > 1:

                def step(earlier, state):
                    result = []
                    for (peak, mixed), tile_q in zip(state, tile_qs):
                        raw = scores(tile_q, keys(pk_ref[earlier], pd_ref[earlier]))
                        higher = jnp.maximum(peak, top(raw))
                        decay = jnp.exp2((peak - higher) * factor)
                        result.append((higher, mixed * decay + mix(raw, higher, values(pv_ref[earlier]))))
                    return result

                low = functools.reduce(jnp.minimum, [low_of(place) for place in places])
                least = jnp.maximum(low + meta_ref[0] * rows, 0) // rows
                mixes = [mixed for _, mixed in lax.fori_loop(least, meta_ref[0], step, list(zip(peaks, mixes)))]
            groups = heads // TOGETHER
            for at, mixed in enumerate(mixes):
                result = (mixed[:, :LANES] / mixed[:, LANES:]).astype(jnp.bfloat16)
                for head in range(TOGETHER):
                    column = (at % groups * TOGETHER + head) * LANES
                    result_ref[indices[at // groups], :, column : column + LANES] = result[head * cap : (head + 1) * cap]

        def body(pair, carry):
            indices = [list_ref[2 * pair], list_ref[2 * pair + 1]]
            places = [place_of(index) for index in indices]
            low = jnp.minimum(*[low_of(place) for place in places])
            short = jnp.maximum(*places) < blocks // 2
            for seen_keys, here in ((half, short), (rows, jnp.logical_not(short))):
                if count > 1:
                    pl.when(here)(functools.partial(some_blocks, indices, places, seen_keys, False))
                else:
                    pl.when(here & (low >= 0))(functools.partial(some_blocks, indices, places, seen_keys, False))
                    pl.when(here & (low < 0))(functools.partial(some_blocks, indices, places, seen_keys, True))
            result_copy(indices[0]).start()
            pl.when(indices[0] != indices[1])(result_copy(indices[1]).start)
            return carry

        held = jnp.int32(0)
        for index in range(parcels):
            list_ref[held] = index
            held += jnp.where(place_of(index) < blocks, 1, 0)
        list_ref[held] = list_ref[jnp.maximum(held - 1, 0)]

        for index in range(parcels):

            @pl.when(place_of(index) < blocks)
            def _():
                stage_ref[index] = array_refs[0][index] if index < slots else array_refs[index - slots + (slots > 0)][...]

        lax.fori_loop(0, (held + 1) // 2, body, 0)
        for index in range(parcels):
            pl.when(place_of(index) < blocks)(result_copy(index).wait)

    operands = [meta, *own, *past, *arrays]
    specs = [SMEM] + [VMEM] * (len(operands) - 1)
    aliases = {}
    if out is not None:
        aliases = {len(operands): 0}
        operands.append(out)
        specs.append(ANY)
    area = max(1, parcels // 2) * heads * cap * (count + 1) * rows
    return pl.pallas_call(
        kernel,
        out_shape=jax.ShapeDtypeStruct((rows, width), jnp.bfloat16),
        in_specs=specs,
        out_specs=ANY,
        input_output_aliases=aliases,
        scratch_shapes=[
            pltpu.VMEM((parcels, cap, width), jnp.bfloat16),
            pltpu.VMEM((parcels, cap, width), jnp.bfloat16),
            pltpu.SMEM((parcels + 1,), jnp.int32),
            pltpu.SemaphoreType.DMA((parcels,)),
        ],
        compiler_params=params(28),
        cost_estimate=pl.CostEstimate(
            flops=8 * area * LANES, bytes_accessed=4 * parcels * cap * width, transcendentals=area
        ),
        name="attend",
    )(*operands)


def digits(begin):
    lane = jnp.arange(LANES, dtype=jnp.int32)
    digit = jnp.where(lane < DIGIT, begin[..., None] // DIGIT, begin[..., None] % DIGIT)
    hit = digit == lane % DIGIT
    return jnp.where(hit, 1.0, 0.0).astype(jnp.bfloat16), jnp.where(hit, 0.0, -APART).astype(jnp.bfloat16)


def local(queries, keys_values, routing, documents):
    rows, width = queries.shape
    owners = lax.axis_size("dp")
    columns = lax.axis_size("ctx")
    kv_heads, pair, head_dim = keys_values.shape[1:]
    assert kv_heads == 1 and pair == 2 and head_dim == LANES
    cap = 2 * rows // owners
    blocks = rows // cap
    seq_len = rows * columns
    assert seq_len <= DIGIT * DIGIT
    half = owners // 2
    assert owners & (owners - 1) == 0
    column = lax.axis_index("ctx")
    me = lax.axis_index("dp")

    routing = routing.T
    send_kv = pack_kv(routing, documents.reshape(-1, LANES), keys_values.reshape(2 * rows, LANES), owners, seq_len)
    parcels = lax.all_to_all(send_kv, "dp", split_axis=0, concat_axis=0, tiled=True)
    near, *far = pack_q(routing, queries, send_kv, owners)
    groups = [list(range(half)), list(range(half, owners))]
    near = lax.all_to_all(near, "dp", split_axis=0, concat_axis=0, axis_index_groups=groups, tiled=True)
    label = parcels[:, :4].astype(jnp.float32).astype(jnp.int32)
    place, part = label[:, 2, 0], label[:, 3, 0]
    begin = (label[:, 0] * DIGIT + label[:, 1]).reshape(owners, LANES // cap, cap)
    slots = jnp.arange(blocks, dtype=jnp.int32)
    every = jnp.arange(owners, dtype=jnp.int32)
    chosen = place[None, :] == slots[:, None]
    source = jnp.sum(jnp.where(chosen, every[None, :], 0), axis=1)
    senders = jnp.concatenate([me // half * half + every[:half], me ^ every[half:]])
    places = jnp.sum(jnp.where(senders[:, None] == every[None, :], place[None, :], 0), axis=1)
    wanted = chosen[:, :, None] & (part[None, :, None] == jnp.arange(LANES // cap, dtype=jnp.int32))
    doc = jnp.sum(jnp.where(wanted[..., None], begin[None], 0), axis=(1, 2)).reshape(rows)

    split = jnp.concatenate([doc // DIGIT, doc % DIGIT]).astype(jnp.float32).astype(jnp.bfloat16).reshape(-1, LANES)
    split = jnp.pad(split, ((0, -split.shape[0] % LABEL_ROWS), (0, 0)))
    own_kv = place_kv(source, parcels, split, rows, cap)
    past_kv = lax.ppermute(own_kv, "ctx", [(0, 1)])[None] if columns == 2 else lax.all_gather(own_kv, "ctx")
    same, apart = digits(doc)
    own = (same, own_kv[: 2 * rows].reshape(rows, 2, LANES)[:, 0], apart, own_kv[: 2 * rows].reshape(rows, 2, LANES)[:, 1])
    past_doc = past_kv[:, 2 * rows :][:, : 2 * rows // LANES].reshape(-1, 2, rows).astype(jnp.float32).astype(jnp.int32)
    past_apart = digits(past_doc[:, 0] * DIGIT + past_doc[:, 1])[1]
    past_rows = past_kv[:, : 2 * rows].reshape(-1, rows, 2, LANES)
    past = (past_rows[:, :, 0], past_apart, past_rows[:, :, 1])

    lows = jnp.min(doc.reshape(blocks, cap), axis=1) - column * rows
    meta = jnp.concatenate([column[None], places, lows])
    sent, far = far, []
    for index, parcel in enumerate(sent):
        if index >= 3:
            ties = (past_kv,) if index >= half - 2 else (far[index - 3], own_kv)
            parcel = lax.optimization_barrier((parcel, *ties))[0]
        far.append(lax.ppermute(parcel, "dp", [(owner, owner ^ (half + index)) for owner in range(owners)]))
    out = attend(meta, half, None, far[: half - 5], own, past, None)
    out = attend(meta, half + half - 5, None, far[half - 5 : half - 2], own, past, out)
    out = attend(meta, 0, near, [], own, past, out)
    return attend(meta, half + half - 2, None, far[half - 2 :], own, past, out)


def solution(mesh):
    placed = (
        P(("dp", "ctx"), None),
        P(("dp", "ctx"), None, None, None),
        P(("dp", "ctx"), None),
        P(("dp", "ctx")),
    )
    return jax.shard_map(
        local, mesh=mesh, in_specs=placed, out_specs=P(("dp", "ctx"), None), check_vma=False
    )
```

```python
import functools
import math

import jax
import jax.numpy as jnp
from jax import lax
from jax.experimental import pallas as pl
from jax.experimental.pallas import tpu as pltpu
from jax.sharding import PartitionSpec as P

LANES = 128
LABEL_ROWS = 16
DIGIT = 64
TOGETHER = 8
APART = 16384.0
NEVER = -1e30
ANY = pl.BlockSpec(memory_space=pl.ANY)
VMEM = pl.BlockSpec(memory_space=pltpu.VMEM)
SMEM = pl.BlockSpec(memory_space=pltpu.SMEM)


def params(mib):
    return pltpu.CompilerParams(vmem_limit_bytes=mib * 1024 * 1024)


def hbm(*arrays):
    return [pltpu.with_memory_space_constraint(array, pltpu.HBM) for array in arrays]


def pack_kv(routing, documents, kv, owners, seq_len):
    rows = kv.shape[0] // 2
    cap = 2 * rows // owners
    blocks = rows // cap
    per_group = LANES // cap

    def kernel(routing_any, doc_any, kv_any, out_ref, routing_ref, doc_ref, kv_ref, label_ref, held_ref, in_sem, sem, label_sem):
        fetches = [
            pltpu.make_async_copy(source, target, in_sem.at[index])
            for index, (source, target) in enumerate(
                ((routing_any, routing_ref), (doc_any, doc_ref), (kv_any, kv_ref))
            )
        ]
        for fetch in fetches:
            fetch.start()
        fetches[0].wait()
        for slot in range(owners):
            held_ref[slot] = blocks
        for block in range(blocks):
            held_ref[routing_ref[0, block * cap]] = block
        fetches[1].wait()
        row_at = lax.broadcasted_iota(jnp.int32, (LABEL_ROWS, LANES), 0)
        label_ref[blocks] = jnp.full((LABEL_ROWS, LANES), 255.0, jnp.bfloat16)
        for block in range(blocks):
            group, part = divmod(block, per_group)
            begin = doc_ref[group : group + 1, :] - routing_ref[0, block * cap] * seq_len
            place = routing_ref[1, block * cap] // cap
            label = jnp.where(row_at == 0, begin // DIGIT, jnp.where(row_at == 1, begin % DIGIT, part))
            label = jnp.where(row_at == 2, place, label)
            label_ref[block] = label.astype(jnp.float32).astype(jnp.bfloat16)
        copies = [
            pltpu.make_async_copy(
                label_ref.at[held_ref[slot]], out_ref.at[slot, pl.ds(0, LABEL_ROWS)], label_sem.at[slot]
            )
            for slot in range(owners)
        ]
        for block in range(blocks):
            copies.append(
                pltpu.make_async_copy(
                    kv_ref.at[pl.ds(block * 2 * cap, 2 * cap)],
                    out_ref.at[routing_ref[0, block * cap], pl.ds(LABEL_ROWS, 2 * cap)],
                    sem.at[block],
                )
            )
        fetches[2].wait()
        for copy in copies:
            copy.start()
        for copy in copies:
            copy.wait()

    return pl.pallas_call(
        kernel,
        out_shape=pltpu.HBM((owners, LABEL_ROWS + 2 * cap, LANES), kv.dtype),
        in_specs=[ANY] * 3,
        out_specs=ANY,
        scratch_shapes=[
            pltpu.SMEM(routing.shape, jnp.int32),
            pltpu.VMEM(documents.shape, jnp.int32),
            pltpu.VMEM(kv.shape, kv.dtype),
            pltpu.VMEM((blocks + 1, LABEL_ROWS, LANES), jnp.bfloat16),
            pltpu.SMEM((owners,), jnp.int32),
            pltpu.SemaphoreType.DMA((3,)),
            pltpu.SemaphoreType.DMA((blocks,)),
            pltpu.SemaphoreType.DMA((owners,)),
        ],
        compiler_params=params(16),
        name="pack_kv",
    )(*hbm(routing, documents, kv))


def pack_q(routing, queries, earlier, owners):
    rows, width = queries.shape
    cap = 2 * rows // owners
    blocks = rows // cap
    half = owners // 2

    def kernel(routing_any, q_any, earlier_ref, near_ref, *rest):
        far_refs = rest[:half]
        routing_ref, q_ref, held_ref, in_sem, q_sem, sem = rest[half:]
        me = lax.axis_index("dp")
        fetch = pltpu.make_async_copy(routing_any, routing_ref, in_sem)
        fetch.start()
        fetch_q = pltpu.make_async_copy(q_any, q_ref, q_sem)
        fetch_q.start()
        fetch.wait()
        for slot in range(owners):
            held_ref[slot] = blocks
        for block in range(blocks):
            held_ref[routing_ref[0, block * cap]] = block
        copies = []
        for step in range(owners):
            slot = me ^ step
            block = held_ref[slot]
            q_rows = pl.ds(pl.multiple_of(jnp.minimum(block, blocks - 1) * cap, cap), cap)
            target = far_refs[step - half] if step >= half else near_ref.at[lax.rem(slot, half)]
            copies.append((block < blocks, pltpu.make_async_copy(q_ref.at[q_rows], target, sem.at[step])))
        fetch_q.wait()
        for held, copy in copies:
            pl.when(held)(copy.start)
        for held, copy in copies:
            pl.when(held)(copy.wait)

    return pl.pallas_call(
        kernel,
        out_shape=[
            pltpu.HBM((half, cap, width), queries.dtype),
            *[jax.ShapeDtypeStruct((cap, width), queries.dtype)] * half,
        ],
        in_specs=[ANY] * 3,
        out_specs=[ANY] * (1 + half),
        scratch_shapes=[
            pltpu.SMEM(routing.shape, jnp.int32),
            pltpu.VMEM(queries.shape, queries.dtype),
            pltpu.SMEM((owners,), jnp.int32),
            pltpu.SemaphoreType.DMA,
            pltpu.SemaphoreType.DMA,
            pltpu.SemaphoreType.DMA((owners,)),
        ],
        compiler_params=params(16),
        name="pack_q",
    )(*hbm(routing, queries, earlier))


def place_kv(source, parcels, begins, rows, cap):
    blocks = rows // cap

    def kernel(source_ref, in_ref, begin_ref, out_ref, sem):
        copies = [
            pltpu.make_async_copy(
                in_ref.at[source_ref[place], pl.ds(LABEL_ROWS, 2 * cap)],
                out_ref.at[pl.ds(place * 2 * cap, 2 * cap)],
                sem.at[place],
            )
            for place in range(blocks)
        ]
        copies.append(
            pltpu.make_async_copy(begin_ref, out_ref.at[pl.ds(2 * rows, begin_ref.shape[0])], sem.at[blocks])
        )
        for copy in copies:
            copy.start()
        for copy in copies:
            copy.wait()

    return pl.pallas_call(
        kernel,
        out_shape=jax.ShapeDtypeStruct((2 * rows + begins.shape[0], LANES), parcels.dtype),
        in_specs=[SMEM, ANY, ANY],
        out_specs=ANY,
        scratch_shapes=[pltpu.SemaphoreType.DMA((blocks + 1,))],
        compiler_params=params(16),
        name="place_kv",
    )(source, parcels, begins)


def attend(meta, first, near, far, own, past, out):
    rows = own[0].shape[0]
    cap, width = near.shape[1:] if far == [] else far[0].shape
    blocks = rows // cap
    heads = width // LANES
    half = rows // 2
    count = past[0].shape[0]
    slots = 0 if near is None else near.shape[0]
    parcels = slots + len(far)
    lows_at = meta.shape[0] - blocks
    factor = math.log2(math.e) / math.sqrt(LANES)
    arrays = ([] if near is None else [near]) + far

    def kernel(meta_ref, qd_ref, ok_ref, od_ref, ov_ref, pk_ref, pd_ref, pv_ref, *rest):
        array_refs = rest[: len(arrays)]
        out_any, stage_ref, result_ref, list_ref, sem = rest[-5:]

        def keys(k_ref, d_ref):
            return jnp.concatenate([k_ref, d_ref], axis=1)

        def values(v):
            return jnp.concatenate([v, jnp.ones(v.shape, v.dtype)], axis=1)

        def scores(tile_q, tile_k):
            return lax.dot_general(tile_q, tile_k, (((1,), (1,)), ((), ())), preferred_element_type=jnp.float32)

        def top(raw):
            return jnp.max(raw, axis=-1, keepdims=True)

        def mix(raw, peak, tile_v):
            weights = jnp.exp2((raw - peak) * factor).astype(jnp.bfloat16)
            return jnp.dot(weights, tile_v, preferred_element_type=jnp.float32)

        def place_of(index):
            return meta_ref[1 + first + index]

        def low_of(place):
            return meta_ref[lows_at + jnp.minimum(place, blocks - 1)]

        def result_copy(index):
            at = pl.multiple_of(jnp.minimum(place_of(index), blocks - 1) * cap, cap)
            return pltpu.make_async_copy(result_ref.at[index], out_any.at[pl.ds(at, cap)], sem.at[index])

        def some_blocks(indices, places, seen_keys, with_past):
            tile_qs, raws = [], []
            for index, place in zip(indices, places):
                block_q = stage_ref[index]
                same = qd_ref[pl.ds(pl.multiple_of(place * cap, cap), cap), :]
                same = jnp.concatenate([same] * TOGETHER, axis=0)
                row_at = lax.broadcasted_iota(jnp.int32, (cap, seen_keys), 0) + place * cap
                seen = lax.broadcasted_iota(jnp.int32, (cap, seen_keys), 1) <= row_at
                for begin in range(0, heads, TOGETHER):
                    tiles = [block_q[:, head * LANES : (head + 1) * LANES] for head in range(begin, begin + TOGETHER)]
                    tile_q = jnp.concatenate([jnp.concatenate(tiles, axis=0), same], axis=1)
                    raw = scores(tile_q, keys(ok_ref[:seen_keys], od_ref[:seen_keys]))
                    raw = jnp.where(seen[None], raw.reshape(TOGETHER, cap, seen_keys), NEVER)
                    tile_qs.append(tile_q)
                    raws.append([raw.reshape(TOGETHER * cap, seen_keys)])
            tile_vs = [ov_ref[:seen_keys]]
            if with_past:
                for several, tile_q in zip(raws, tile_qs):
                    several.append(scores(tile_q, keys(pk_ref[0], pd_ref[0])))
                tile_vs.append(pv_ref[0])
            peaks = [functools.reduce(jnp.maximum, [top(raw) for raw in several]) for several in raws]
            mixes = [
                sum(mix(raw, peak, values(tile_v)) for raw, tile_v in zip(several, tile_vs))
                for several, peak in zip(raws, peaks)
            ]
            if count > 1:

                def step(earlier, state):
                    result = []
                    for (peak, mixed), tile_q in zip(state, tile_qs):
                        raw = scores(tile_q, keys(pk_ref[earlier], pd_ref[earlier]))
                        higher = jnp.maximum(peak, top(raw))
                        decay = jnp.exp2((peak - higher) * factor)
                        result.append((higher, mixed * decay + mix(raw, higher, values(pv_ref[earlier]))))
                    return result

                low = functools.reduce(jnp.minimum, [low_of(place) for place in places])
                least = jnp.maximum(low + meta_ref[0] * rows, 0) // rows
                mixes = [mixed for _, mixed in lax.fori_loop(least, meta_ref[0], step, list(zip(peaks, mixes)))]
            groups = heads // TOGETHER
            for at, mixed in enumerate(mixes):
                result = (mixed[:, :LANES] / mixed[:, LANES:]).astype(jnp.bfloat16)
                for head in range(TOGETHER):
                    column = (at % groups * TOGETHER + head) * LANES
                    result_ref[indices[at // groups], :, column : column + LANES] = result[head * cap : (head + 1) * cap]

        def body(pair, carry):
            indices = [list_ref[2 * pair], list_ref[2 * pair + 1]]
            places = [place_of(index) for index in indices]
            low = jnp.minimum(*[low_of(place) for place in places])
            short = jnp.maximum(*places) < blocks // 2
            for seen_keys, here in ((half, short), (rows, jnp.logical_not(short))):
                if count > 1:
                    pl.when(here)(functools.partial(some_blocks, indices, places, seen_keys, False))
                else:
                    pl.when(here & (low >= 0))(functools.partial(some_blocks, indices, places, seen_keys, False))
                    pl.when(here & (low < 0))(functools.partial(some_blocks, indices, places, seen_keys, True))
            result_copy(indices[0]).start()
            pl.when(indices[0] != indices[1])(result_copy(indices[1]).start)
            return carry

        held = jnp.int32(0)
        for index in range(parcels):
            list_ref[held] = index
            held += jnp.where(place_of(index) < blocks, 1, 0)
        list_ref[held] = list_ref[jnp.maximum(held - 1, 0)]

        for index in range(parcels):

            @pl.when(place_of(index) < blocks)
            def _():
                stage_ref[index] = array_refs[0][index] if index < slots else array_refs[index - slots + (slots > 0)][...]

        lax.fori_loop(0, (held + 1) // 2, body, 0)
        for index in range(parcels):
            pl.when(place_of(index) < blocks)(result_copy(index).wait)

    operands = [meta, *own, *past, *arrays]
    specs = [SMEM] + [VMEM] * (len(operands) - 1)
    aliases = {}
    if out is not None:
        aliases = {len(operands): 0}
        operands.append(out)
        specs.append(ANY)
    area = max(1, parcels // 2) * heads * cap * (count + 1) * rows
    return pl.pallas_call(
        kernel,
        out_shape=jax.ShapeDtypeStruct((rows, width), jnp.bfloat16),
        in_specs=specs,
        out_specs=ANY,
        input_output_aliases=aliases,
        scratch_shapes=[
            pltpu.VMEM((parcels, cap, width), jnp.bfloat16),
            pltpu.VMEM((parcels, cap, width), jnp.bfloat16),
            pltpu.SMEM((parcels + 1,), jnp.int32),
            pltpu.SemaphoreType.DMA((parcels,)),
        ],
        compiler_params=params(28),
        cost_estimate=pl.CostEstimate(
            flops=8 * area * LANES, bytes_accessed=4 * parcels * cap * width, transcendentals=area
        ),
        name="attend",
    )(*operands)


def digits(begin):
    lane = jnp.arange(LANES, dtype=jnp.int32)
    digit = jnp.where(lane < DIGIT, begin[..., None] // DIGIT, begin[..., None] % DIGIT)
    hit = digit == lane % DIGIT
    return jnp.where(hit, 1.0, 0.0).astype(jnp.bfloat16), jnp.where(hit, 0.0, -APART).astype(jnp.bfloat16)


def local(queries, keys_values, routing, documents):
    rows, width = queries.shape
    owners = lax.axis_size("dp")
    columns = lax.axis_size("ctx")
    kv_heads, pair, head_dim = keys_values.shape[1:]
    assert kv_heads == 1 and pair == 2 and head_dim == LANES
    cap = 2 * rows // owners
    blocks = rows // cap
    seq_len = rows * columns
    assert seq_len <= DIGIT * DIGIT
    half = owners // 2
    assert owners & (owners - 1) == 0
    column = lax.axis_index("ctx")
    me = lax.axis_index("dp")

    routing = routing.T
    send_kv = pack_kv(routing, documents.reshape(-1, LANES), keys_values.reshape(2 * rows, LANES), owners, seq_len)
    parcels = lax.all_to_all(send_kv, "dp", split_axis=0, concat_axis=0, tiled=True)
    near, *far = pack_q(routing, queries, send_kv, owners)
    groups = [list(range(half)), list(range(half, owners))]
    near = lax.all_to_all(near, "dp", split_axis=0, concat_axis=0, axis_index_groups=groups, tiled=True)
    label = parcels[:, :4].astype(jnp.float32).astype(jnp.int32)
    place, part = label[:, 2, 0], label[:, 3, 0]
    begin = (label[:, 0] * DIGIT + label[:, 1]).reshape(owners, LANES // cap, cap)
    slots = jnp.arange(blocks, dtype=jnp.int32)
    every = jnp.arange(owners, dtype=jnp.int32)
    chosen = place[None, :] == slots[:, None]
    source = jnp.sum(jnp.where(chosen, every[None, :], 0), axis=1)
    senders = jnp.concatenate([me // half * half + every[:half], me ^ every[half:]])
    places = jnp.sum(jnp.where(senders[:, None] == every[None, :], place[None, :], 0), axis=1)
    wanted = chosen[:, :, None] & (part[None, :, None] == jnp.arange(LANES // cap, dtype=jnp.int32))
    doc = jnp.sum(jnp.where(wanted[..., None], begin[None], 0), axis=(1, 2)).reshape(rows)

    split = jnp.concatenate([doc // DIGIT, doc % DIGIT]).astype(jnp.float32).astype(jnp.bfloat16).reshape(-1, LANES)
    split = jnp.pad(split, ((0, -split.shape[0] % LABEL_ROWS), (0, 0)))
    own_kv = place_kv(source, parcels, split, rows, cap)
    past_kv = lax.ppermute(own_kv, "ctx", [(0, 1)])[None] if columns == 2 else lax.all_gather(own_kv, "ctx")
    same, apart = digits(doc)
    own = (same, own_kv[: 2 * rows].reshape(rows, 2, LANES)[:, 0], apart, own_kv[: 2 * rows].reshape(rows, 2, LANES)[:, 1])
    past_doc = past_kv[:, 2 * rows :][:, : 2 * rows // LANES].reshape(-1, 2, rows).astype(jnp.float32).astype(jnp.int32)
    past_apart = digits(past_doc[:, 0] * DIGIT + past_doc[:, 1])[1]
    past_rows = past_kv[:, : 2 * rows].reshape(-1, rows, 2, LANES)
    past = (past_rows[:, :, 0], past_apart, past_rows[:, :, 1])

    lows = jnp.min(doc.reshape(blocks, cap), axis=1) - column * rows
    meta = jnp.concatenate([column[None], places, lows])
    sent, far = far, []
    for index, parcel in enumerate(sent):
        if index >= 4:
            ties = (past_kv,) if index >= half - 2 else (far[index - 4], own_kv)
            parcel = lax.optimization_barrier((parcel, *ties))[0]
        far.append(lax.ppermute(parcel, "dp", [(owner, owner ^ (half + index)) for owner in range(owners)]))
    out = attend(meta, half, None, far[: half - 5], own, past, None)
    out = attend(meta, half + half - 5, None, far[half - 5 : half - 2], own, past, out)
    out = attend(meta, 0, near, [], own, past, out)
    return attend(meta, half + half - 2, None, far[half - 2 :], own, past, out)


def solution(mesh):
    placed = (
        P(("dp", "ctx"), None),
        P(("dp", "ctx"), None, None, None),
        P(("dp", "ctx"), None),
        P(("dp", "ctx")),
    )
    return jax.shard_map(
        local, mesh=mesh, in_specs=placed, out_specs=P(("dp", "ctx"), None), check_vma=False
    )
```

```python
import functools
import math

import jax
import jax.numpy as jnp
from jax import lax
from jax.experimental import pallas as pl
from jax.experimental.pallas import tpu as pltpu
from jax.sharding import PartitionSpec as P

LANES = 128
LABEL_ROWS = 16
DIGIT = 64
TOGETHER = 4
APART = 16384.0
NEVER = -1e30
ANY = pl.BlockSpec(memory_space=pl.ANY)
VMEM = pl.BlockSpec(memory_space=pltpu.VMEM)
SMEM = pl.BlockSpec(memory_space=pltpu.SMEM)


def params(mib):
    return pltpu.CompilerParams(vmem_limit_bytes=mib * 1024 * 1024)


def hbm(*arrays):
    return [pltpu.with_memory_space_constraint(array, pltpu.HBM) for array in arrays]


def pack_kv(routing, documents, kv, owners, seq_len):
    rows = kv.shape[0] // 2
    cap = 2 * rows // owners
    blocks = rows // cap
    per_group = LANES // cap

    def kernel(routing_any, doc_any, kv_any, out_ref, routing_ref, doc_ref, kv_ref, label_ref, held_ref, in_sem, sem, label_sem):
        fetches = [
            pltpu.make_async_copy(source, target, in_sem.at[index])
            for index, (source, target) in enumerate(
                ((routing_any, routing_ref), (doc_any, doc_ref), (kv_any, kv_ref))
            )
        ]
        for fetch in fetches:
            fetch.start()
        fetches[0].wait()
        for slot in range(owners):
            held_ref[slot] = blocks
        for block in range(blocks):
            held_ref[routing_ref[0, block * cap]] = block
        copies = []
        for block in range(blocks):
            copies.append(
                pltpu.make_async_copy(
                    kv_ref.at[pl.ds(block * 2 * cap, 2 * cap)],
                    out_ref.at[routing_ref[0, block * cap], pl.ds(LABEL_ROWS, 2 * cap)],
                    sem.at[block],
                )
            )
        fetches[2].wait()
        for copy in copies:
            copy.start()
        fetches[1].wait()
        row_at = lax.broadcasted_iota(jnp.int32, (LABEL_ROWS, LANES), 0)
        label_ref[blocks] = jnp.full((LABEL_ROWS, LANES), 255.0, jnp.bfloat16)
        for block in range(blocks):
            group, part = divmod(block, per_group)
            begin = doc_ref[group : group + 1, :] - routing_ref[0, block * cap] * seq_len
            place = routing_ref[1, block * cap] // cap
            label = jnp.where(row_at == 0, begin // DIGIT, jnp.where(row_at == 1, begin % DIGIT, part))
            label = jnp.where(row_at == 2, place, label)
            label_ref[block] = label.astype(jnp.float32).astype(jnp.bfloat16)
        labels = [
            pltpu.make_async_copy(
                label_ref.at[held_ref[slot]], out_ref.at[slot, pl.ds(0, LABEL_ROWS)], label_sem.at[slot]
            )
            for slot in range(owners)
        ]
        for label in labels:
            label.start()
        for copy in copies + labels:
            copy.wait()

    return pl.pallas_call(
        kernel,
        out_shape=pltpu.HBM((owners, LABEL_ROWS + 2 * cap, LANES), kv.dtype),
        in_specs=[ANY] * 3,
        out_specs=ANY,
        scratch_shapes=[
            pltpu.SMEM(routing.shape, jnp.int32),
            pltpu.VMEM(documents.shape, jnp.int32),
            pltpu.VMEM(kv.shape, kv.dtype),
            pltpu.VMEM((blocks + 1, LABEL_ROWS, LANES), jnp.bfloat16),
            pltpu.SMEM((owners,), jnp.int32),
            pltpu.SemaphoreType.DMA((3,)),
            pltpu.SemaphoreType.DMA((blocks,)),
            pltpu.SemaphoreType.DMA((owners,)),
        ],
        compiler_params=params(16),
        name="pack_kv",
    )(*hbm(routing, documents, kv))


def pack_q(routing, queries, earlier, owners):
    rows, width = queries.shape
    cap = 2 * rows // owners
    blocks = rows // cap
    half = owners // 2

    def kernel(routing_any, q_any, earlier_ref, near_ref, *rest):
        far_refs = rest[:half]
        routing_ref, q_ref, held_ref, in_sem, q_sem, sem = rest[half:]
        me = lax.axis_index("dp")
        fetch = pltpu.make_async_copy(routing_any, routing_ref, in_sem)
        fetch.start()
        fetch_q = pltpu.make_async_copy(q_any, q_ref, q_sem)
        fetch_q.start()
        fetch.wait()
        for slot in range(owners):
            held_ref[slot] = blocks
        for block in range(blocks):
            held_ref[routing_ref[0, block * cap]] = block
        copies = []
        for step in range(owners):
            slot = me ^ step
            block = held_ref[slot]
            q_rows = pl.ds(pl.multiple_of(jnp.minimum(block, blocks - 1) * cap, cap), cap)
            target = far_refs[step - half] if step >= half else near_ref.at[lax.rem(slot, half)]
            copies.append((block < blocks, pltpu.make_async_copy(q_ref.at[q_rows], target, sem.at[step])))
        fetch_q.wait()
        for held, copy in copies:
            pl.when(held)(copy.start)
        for held, copy in copies:
            pl.when(held)(copy.wait)

    return pl.pallas_call(
        kernel,
        out_shape=[
            pltpu.HBM((half, cap, width), queries.dtype),
            *[jax.ShapeDtypeStruct((cap, width), queries.dtype)] * half,
        ],
        in_specs=[ANY] * 3,
        out_specs=[ANY] * (1 + half),
        scratch_shapes=[
            pltpu.SMEM(routing.shape, jnp.int32),
            pltpu.VMEM(queries.shape, queries.dtype),
            pltpu.SMEM((owners,), jnp.int32),
            pltpu.SemaphoreType.DMA,
            pltpu.SemaphoreType.DMA,
            pltpu.SemaphoreType.DMA((owners,)),
        ],
        compiler_params=params(16),
        name="pack_q",
    )(*hbm(routing, queries, earlier))


def place_kv(source, parcels, begins, rows, cap):
    blocks = rows // cap

    def kernel(source_ref, in_ref, begin_ref, out_ref, sem):
        copies = [
            pltpu.make_async_copy(
                in_ref.at[source_ref[place], pl.ds(LABEL_ROWS, 2 * cap)],
                out_ref.at[pl.ds(place * 2 * cap, 2 * cap)],
                sem.at[place],
            )
            for place in range(blocks)
        ]
        copies.append(
            pltpu.make_async_copy(begin_ref, out_ref.at[pl.ds(2 * rows, begin_ref.shape[0])], sem.at[blocks])
        )
        for copy in copies:
            copy.start()
        for copy in copies:
            copy.wait()

    return pl.pallas_call(
        kernel,
        out_shape=jax.ShapeDtypeStruct((2 * rows + begins.shape[0], LANES), parcels.dtype),
        in_specs=[SMEM, ANY, ANY],
        out_specs=ANY,
        scratch_shapes=[pltpu.SemaphoreType.DMA((blocks + 1,))],
        compiler_params=params(16),
        name="place_kv",
    )(source, parcels, begins)


def attend(meta, first, near, far, own, past, out):
    rows = own[0].shape[0]
    cap, width = near.shape[1:] if far == [] else far[0].shape
    blocks = rows // cap
    heads = width // LANES
    half = rows // 2
    count = past[0].shape[0]
    slots = 0 if near is None else near.shape[0]
    parcels = slots + len(far)
    lows_at = meta.shape[0] - blocks
    factor = math.log2(math.e) / math.sqrt(LANES)
    arrays = ([] if near is None else [near]) + far

    def kernel(meta_ref, qd_ref, ok_ref, od_ref, ov_ref, pk_ref, pd_ref, pv_ref, *rest):
        array_refs = rest[: len(arrays)]
        out_any, stage_ref, result_ref, list_ref, sem = rest[-5:]

        def keys(k_ref, d_ref):
            return jnp.concatenate([k_ref, d_ref], axis=1)

        def values(v):
            return jnp.concatenate([v, jnp.ones(v.shape, v.dtype)], axis=1)

        def scores(tile_q, tile_k):
            return lax.dot_general(tile_q, tile_k, (((1,), (1,)), ((), ())), preferred_element_type=jnp.float32)

        def top(raw):
            return jnp.max(raw, axis=-1, keepdims=True)

        def mix(raw, peak, tile_v):
            weights = jnp.exp2((raw - peak) * factor).astype(jnp.bfloat16)
            return jnp.dot(weights, tile_v, preferred_element_type=jnp.float32)

        def place_of(index):
            return meta_ref[1 + first + index]

        def low_of(place):
            return meta_ref[lows_at + jnp.minimum(place, blocks - 1)]

        def result_copy(index):
            at = pl.multiple_of(jnp.minimum(place_of(index), blocks - 1) * cap, cap)
            return pltpu.make_async_copy(result_ref.at[index], out_any.at[pl.ds(at, cap)], sem.at[index])

        def some_blocks(indices, places, seen_keys, with_past):
            tile_qs, raws = [], []
            for index, place in zip(indices, places):
                block_q = stage_ref[index]
                same = qd_ref[pl.ds(pl.multiple_of(place * cap, cap), cap), :]
                same = jnp.concatenate([same] * TOGETHER, axis=0)
                row_at = lax.broadcasted_iota(jnp.int32, (cap, seen_keys), 0) + place * cap
                seen = lax.broadcasted_iota(jnp.int32, (cap, seen_keys), 1) <= row_at
                for begin in range(0, heads, TOGETHER):
                    tiles = [block_q[:, head * LANES : (head + 1) * LANES] for head in range(begin, begin + TOGETHER)]
                    tile_q = jnp.concatenate([jnp.concatenate(tiles, axis=0), same], axis=1)
                    raw = scores(tile_q, keys(ok_ref[:seen_keys], od_ref[:seen_keys]))
                    raw = jnp.where(seen[None], raw.reshape(TOGETHER, cap, seen_keys), NEVER)
                    tile_qs.append(tile_q)
                    raws.append([raw.reshape(TOGETHER * cap, seen_keys)])
            tile_vs = [ov_ref[:seen_keys]]
            if with_past:
                for several, tile_q in zip(raws, tile_qs):
                    several.append(scores(tile_q, keys(pk_ref[0], pd_ref[0])))
                tile_vs.append(pv_ref[0])
            peaks = [functools.reduce(jnp.maximum, [top(raw) for raw in several]) for several in raws]
            mixes = [
                sum(mix(raw, peak, values(tile_v)) for raw, tile_v in zip(several, tile_vs))
                for several, peak in zip(raws, peaks)
            ]
            if count > 1:

                def step(earlier, state):
                    result = []
                    for (peak, mixed), tile_q in zip(state, tile_qs):
                        raw = scores(tile_q, keys(pk_ref[earlier], pd_ref[earlier]))
                        higher = jnp.maximum(peak, top(raw))
                        decay = jnp.exp2((peak - higher) * factor)
                        result.append((higher, mixed * decay + mix(raw, higher, values(pv_ref[earlier]))))
                    return result

                low = functools.reduce(jnp.minimum, [low_of(place) for place in places])
                least = jnp.maximum(low + meta_ref[0] * rows, 0) // rows
                mixes = [mixed for _, mixed in lax.fori_loop(least, meta_ref[0], step, list(zip(peaks, mixes)))]
            groups = heads // TOGETHER
            for at, mixed in enumerate(mixes):
                result = (mixed[:, :LANES] / mixed[:, LANES:]).astype(jnp.bfloat16)
                for head in range(TOGETHER):
                    column = (at % groups * TOGETHER + head) * LANES
                    result_ref[indices[at // groups], :, column : column + LANES] = result[head * cap : (head + 1) * cap]

        def body(pair, carry):
            indices = [list_ref[2 * pair], list_ref[2 * pair + 1]]
            places = [place_of(index) for index in indices]
            low = jnp.minimum(*[low_of(place) for place in places])
            short = jnp.maximum(*places) < blocks // 2
            for seen_keys, here in ((half, short), (rows, jnp.logical_not(short))):
                if count > 1:
                    pl.when(here)(functools.partial(some_blocks, indices, places, seen_keys, False))
                else:
                    pl.when(here & (low >= 0))(functools.partial(some_blocks, indices, places, seen_keys, False))
                    pl.when(here & (low < 0))(functools.partial(some_blocks, indices, places, seen_keys, True))
            result_copy(indices[0]).start()
            pl.when(indices[0] != indices[1])(result_copy(indices[1]).start)
            return carry

        held = jnp.int32(0)
        for index in range(parcels):
            list_ref[held] = index
            held += jnp.where(place_of(index) < blocks, 1, 0)
        list_ref[held] = list_ref[jnp.maximum(held - 1, 0)]

        for index in range(parcels):

            @pl.when(place_of(index) < blocks)
            def _():
                stage_ref[index] = array_refs[0][index] if index < slots else array_refs[index - slots + (slots > 0)][...]

        lax.fori_loop(0, (held + 1) // 2, body, 0)
        for index in range(parcels):
            pl.when(place_of(index) < blocks)(result_copy(index).wait)

    operands = [meta, *own, *past, *arrays]
    specs = [SMEM] + [VMEM] * (len(operands) - 1)
    aliases = {}
    if out is not None:
        aliases = {len(operands): 0}
        operands.append(out)
        specs.append(ANY)
    area = max(1, parcels // 2) * heads * cap * (count + 1) * rows
    return pl.pallas_call(
        kernel,
        out_shape=jax.ShapeDtypeStruct((rows, width), jnp.bfloat16),
        in_specs=specs,
        out_specs=ANY,
        input_output_aliases=aliases,
        scratch_shapes=[
            pltpu.VMEM((parcels, cap, width), jnp.bfloat16),
            pltpu.VMEM((parcels, cap, width), jnp.bfloat16),
            pltpu.SMEM((parcels + 1,), jnp.int32),
            pltpu.SemaphoreType.DMA((parcels,)),
        ],
        compiler_params=params(28),
        cost_estimate=pl.CostEstimate(
            flops=8 * area * LANES, bytes_accessed=4 * parcels * cap * width, transcendentals=area
        ),
        name="attend",
    )(*operands)


def digits(begin):
    lane = jnp.arange(LANES, dtype=jnp.int32)
    digit = jnp.where(lane < DIGIT, begin[..., None] // DIGIT, begin[..., None] % DIGIT)
    hit = digit == lane % DIGIT
    return jnp.where(hit, 1.0, 0.0).astype(jnp.bfloat16), jnp.where(hit, 0.0, -APART).astype(jnp.bfloat16)


def local(queries, keys_values, routing, documents):
    rows, width = queries.shape
    owners = lax.axis_size("dp")
    columns = lax.axis_size("ctx")
    kv_heads, pair, head_dim = keys_values.shape[1:]
    assert kv_heads == 1 and pair == 2 and head_dim == LANES
    cap = 2 * rows // owners
    blocks = rows // cap
    seq_len = rows * columns
    assert seq_len <= DIGIT * DIGIT
    half = owners // 2
    assert owners & (owners - 1) == 0
    column = lax.axis_index("ctx")
    me = lax.axis_index("dp")

    routing = routing.T
    send_kv = pack_kv(routing, documents.reshape(-1, LANES), keys_values.reshape(2 * rows, LANES), owners, seq_len)
    parcels = lax.all_to_all(send_kv, "dp", split_axis=0, concat_axis=0, tiled=True)
    near, *far = pack_q(routing, queries, send_kv, owners)
    groups = [list(range(half)), list(range(half, owners))]
    near = lax.all_to_all(near, "dp", split_axis=0, concat_axis=0, axis_index_groups=groups, tiled=True)
    label = parcels[:, :4].astype(jnp.float32).astype(jnp.int32)
    place, part = label[:, 2, 0], label[:, 3, 0]
    begin = (label[:, 0] * DIGIT + label[:, 1]).reshape(owners, LANES // cap, cap)
    slots = jnp.arange(blocks, dtype=jnp.int32)
    every = jnp.arange(owners, dtype=jnp.int32)
    chosen = place[None, :] == slots[:, None]
    source = jnp.sum(jnp.where(chosen, every[None, :], 0), axis=1)
    senders = jnp.concatenate([me // half * half + every[:half], me ^ every[half:]])
    places = jnp.sum(jnp.where(senders[:, None] == every[None, :], place[None, :], 0), axis=1)
    wanted = chosen[:, :, None] & (part[None, :, None] == jnp.arange(LANES // cap, dtype=jnp.int32))
    doc = jnp.sum(jnp.where(wanted[..., None], begin[None], 0), axis=(1, 2)).reshape(rows)

    split = jnp.concatenate([doc // DIGIT, doc % DIGIT]).astype(jnp.float32).astype(jnp.bfloat16).reshape(-1, LANES)
    split = jnp.pad(split, ((0, -split.shape[0] % LABEL_ROWS), (0, 0)))
    own_kv = place_kv(source, parcels, split, rows, cap)
    past_kv = lax.ppermute(own_kv, "ctx", [(0, 1)])[None] if columns == 2 else lax.all_gather(own_kv, "ctx")
    same, apart = digits(doc)
    own = (same, own_kv[: 2 * rows].reshape(rows, 2, LANES)[:, 0], apart, own_kv[: 2 * rows].reshape(rows, 2, LANES)[:, 1])
    past_doc = past_kv[:, 2 * rows :][:, : 2 * rows // LANES].reshape(-1, 2, rows).astype(jnp.float32).astype(jnp.int32)
    past_apart = digits(past_doc[:, 0] * DIGIT + past_doc[:, 1])[1]
    past_rows = past_kv[:, : 2 * rows].reshape(-1, rows, 2, LANES)
    past = (past_rows[:, :, 0], past_apart, past_rows[:, :, 1])

    lows = jnp.min(doc.reshape(blocks, cap), axis=1) - column * rows
    meta = jnp.concatenate([column[None], places, lows])
    sent, far = far, []
    for index, parcel in enumerate(sent):
        if index >= 4:
            ties = (past_kv,) if index >= half - 2 else (far[index - 4], own_kv)
            parcel = lax.optimization_barrier((parcel, *ties))[0]
        far.append(lax.ppermute(parcel, "dp", [(owner, owner ^ (half + index)) for owner in range(owners)]))
    out = attend(meta, half, None, far[: half - 5], own, past, None)
    out = attend(meta, half + half - 5, None, far[half - 5 : half - 2], own, past, out)
    out = attend(meta, 0, near, [], own, past, out)
    return attend(meta, half + half - 2, None, far[half - 2 :], own, past, out)


def solution(mesh):
    placed = (
        P(("dp", "ctx"), None),
        P(("dp", "ctx"), None, None, None),
        P(("dp", "ctx"), None),
        P(("dp", "ctx")),
    )
    return jax.shard_map(
        local, mesh=mesh, in_specs=placed, out_specs=P(("dp", "ctx"), None), check_vma=False
    )
```

```python
import functools
import math

import jax
import jax.numpy as jnp
from jax import lax
from jax.experimental import pallas as pl
from jax.experimental.pallas import tpu as pltpu
from jax.sharding import PartitionSpec as P

LANES = 128
LABEL_ROWS = 16
DIGIT = 64
TOGETHER = 4
APART = 16384.0
NEVER = -1e30
ANY = pl.BlockSpec(memory_space=pl.ANY)
VMEM = pl.BlockSpec(memory_space=pltpu.VMEM)
SMEM = pl.BlockSpec(memory_space=pltpu.SMEM)


def params(mib):
    return pltpu.CompilerParams(vmem_limit_bytes=mib * 1024 * 1024)


def hbm(*arrays):
    return [pltpu.with_memory_space_constraint(array, pltpu.HBM) for array in arrays]


def pack_kv(routing, documents, kv, owners, seq_len):
    rows = kv.shape[0] // 2
    cap = 2 * rows // owners
    blocks = rows // cap
    per_group = LANES // cap

    def kernel(routing_any, doc_any, kv_any, out_ref, routing_ref, doc_ref, kv_ref, label_ref, held_ref, in_sem, sem, label_sem):
        fetches = [
            pltpu.make_async_copy(source, target, in_sem.at[index])
            for index, (source, target) in enumerate(
                ((routing_any, routing_ref), (doc_any, doc_ref), (kv_any, kv_ref))
            )
        ]
        for fetch in fetches:
            fetch.start()
        fetches[0].wait()
        for slot in range(owners):
            held_ref[slot] = blocks
        for block in range(blocks):
            held_ref[routing_ref[0, block * cap]] = block
        copies = []
        for block in range(blocks):
            copies.append(
                pltpu.make_async_copy(
                    kv_ref.at[pl.ds(block * 2 * cap, 2 * cap)],
                    out_ref.at[routing_ref[0, block * cap], pl.ds(LABEL_ROWS, 2 * cap)],
                    sem.at[block],
                )
            )
        fetches[2].wait()
        for copy in copies:
            copy.start()
        fetches[1].wait()
        row_at = lax.broadcasted_iota(jnp.int32, (LABEL_ROWS, LANES), 0)
        label_ref[blocks] = jnp.full((LABEL_ROWS, LANES), 255.0, jnp.bfloat16)
        for block in range(blocks):
            group, part = divmod(block, per_group)
            begin = doc_ref[group : group + 1, :] - routing_ref[0, block * cap] * seq_len
            place = routing_ref[1, block * cap] // cap
            label = jnp.where(row_at == 0, begin // DIGIT, jnp.where(row_at == 1, begin % DIGIT, part))
            label = jnp.where(row_at == 2, place, label)
            label_ref[block] = label.astype(jnp.float32).astype(jnp.bfloat16)
        labels = [
            pltpu.make_async_copy(
                label_ref.at[held_ref[slot]], out_ref.at[slot, pl.ds(0, LABEL_ROWS)], label_sem.at[slot]
            )
            for slot in range(owners)
        ]
        for label in labels:
            label.start()
        for copy in copies + labels:
            copy.wait()

    return pl.pallas_call(
        kernel,
        out_shape=pltpu.HBM((owners, LABEL_ROWS + 2 * cap, LANES), kv.dtype),
        in_specs=[ANY] * 3,
        out_specs=ANY,
        scratch_shapes=[
            pltpu.SMEM(routing.shape, jnp.int32),
            pltpu.VMEM(documents.shape, jnp.int32),
            pltpu.VMEM(kv.shape, kv.dtype),
            pltpu.VMEM((blocks + 1, LABEL_ROWS, LANES), jnp.bfloat16),
            pltpu.SMEM((owners,), jnp.int32),
            pltpu.SemaphoreType.DMA((3,)),
            pltpu.SemaphoreType.DMA((blocks,)),
            pltpu.SemaphoreType.DMA((owners,)),
        ],
        compiler_params=params(16),
        name="pack_kv",
    )(*hbm(routing, documents, kv))


def pack_q(routing, queries, earlier, owners):
    rows, width = queries.shape
    cap = 2 * rows // owners
    blocks = rows // cap
    half = owners // 2

    def kernel(routing_any, q_any, earlier_ref, near_ref, *rest):
        far_refs = rest[:half]
        routing_ref, q_ref, held_ref, in_sem, q_sem, sem = rest[half:]
        me = lax.axis_index("dp")
        fetch = pltpu.make_async_copy(routing_any, routing_ref, in_sem)
        fetch.start()
        fetch_q = pltpu.make_async_copy(q_any, q_ref, q_sem)
        fetch_q.start()
        fetch.wait()
        for slot in range(owners):
            held_ref[slot] = blocks
        for block in range(blocks):
            held_ref[routing_ref[0, block * cap]] = block
        copies = []
        for step in range(owners):
            slot = me ^ step
            block = held_ref[slot]
            q_rows = pl.ds(pl.multiple_of(jnp.minimum(block, blocks - 1) * cap, cap), cap)
            target = far_refs[step - half] if step >= half else near_ref.at[lax.rem(slot, half)]
            copies.append((block < blocks, pltpu.make_async_copy(q_ref.at[q_rows], target, sem.at[step])))
        fetch_q.wait()
        for held, copy in copies:
            pl.when(held)(copy.start)
        for held, copy in copies:
            pl.when(held)(copy.wait)

    return pl.pallas_call(
        kernel,
        out_shape=[
            pltpu.HBM((half, cap, width), queries.dtype),
            *[jax.ShapeDtypeStruct((cap, width), queries.dtype)] * half,
        ],
        in_specs=[ANY] * 3,
        out_specs=[ANY] * (1 + half),
        scratch_shapes=[
            pltpu.SMEM(routing.shape, jnp.int32),
            pltpu.VMEM(queries.shape, queries.dtype),
            pltpu.SMEM((owners,), jnp.int32),
            pltpu.SemaphoreType.DMA,
            pltpu.SemaphoreType.DMA,
            pltpu.SemaphoreType.DMA((owners,)),
        ],
        compiler_params=params(16),
        name="pack_q",
    )(*hbm(routing, queries, earlier))


def place_kv(source, parcels, begins, rows, cap):
    blocks = rows // cap

    def kernel(source_ref, in_ref, begin_ref, out_ref, sem):
        copies = [
            pltpu.make_async_copy(
                in_ref.at[source_ref[place], pl.ds(LABEL_ROWS, 2 * cap)],
                out_ref.at[pl.ds(place * 2 * cap, 2 * cap)],
                sem.at[place],
            )
            for place in range(blocks)
        ]
        copies.append(
            pltpu.make_async_copy(begin_ref, out_ref.at[pl.ds(2 * rows, begin_ref.shape[0])], sem.at[blocks])
        )
        for copy in copies:
            copy.start()
        for copy in copies:
            copy.wait()

    return pl.pallas_call(
        kernel,
        out_shape=jax.ShapeDtypeStruct((2 * rows + begins.shape[0], LANES), parcels.dtype),
        in_specs=[SMEM, ANY, ANY],
        out_specs=ANY,
        scratch_shapes=[pltpu.SemaphoreType.DMA((blocks + 1,))],
        compiler_params=params(16),
        name="place_kv",
    )(source, parcels, begins)


def attend(meta, first, near, far, own, past, out):
    rows = own[0].shape[0]
    cap, width = near.shape[1:] if far == [] else far[0].shape
    blocks = rows // cap
    heads = width // LANES
    half = rows // 2
    count = past[0].shape[0]
    slots = 0 if near is None else near.shape[0]
    parcels = slots + len(far)
    lows_at = meta.shape[0] - blocks
    factor = math.log2(math.e) / math.sqrt(LANES)
    arrays = ([] if near is None else [near]) + far

    def kernel(meta_ref, qd_ref, ok_ref, od_ref, ov_ref, pk_ref, pd_ref, pv_ref, *rest):
        array_refs = rest[: len(arrays)]
        out_any, stage_ref, result_ref, list_ref, sem = rest[-5:]

        def keys(k_ref, d_ref):
            return jnp.concatenate([k_ref, d_ref], axis=1)

        def values(v):
            return jnp.concatenate([v, jnp.ones(v.shape, v.dtype)], axis=1)

        def scores(tile_q, tile_k):
            return lax.dot_general(tile_q, tile_k, (((1,), (1,)), ((), ())), preferred_element_type=jnp.float32)

        def top(raw):
            return jnp.max(raw, axis=-1, keepdims=True)

        def mix(raw, peak, tile_v):
            weights = jnp.exp2((raw - peak) * factor).astype(jnp.bfloat16)
            return jnp.dot(weights, tile_v, preferred_element_type=jnp.float32)

        def place_of(index):
            return meta_ref[1 + first + index]

        def low_of(place):
            return meta_ref[lows_at + jnp.minimum(place, blocks - 1)]

        def result_copy(index):
            at = pl.multiple_of(jnp.minimum(place_of(index), blocks - 1) * cap, cap)
            return pltpu.make_async_copy(result_ref.at[index], out_any.at[pl.ds(at, cap)], sem.at[index])

        def some_blocks(indices, places, seen_keys, with_past):
            tile_qs, raws = [], []
            for index, place in zip(indices, places):
                block_q = stage_ref[index]
                same = qd_ref[pl.ds(pl.multiple_of(place * cap, cap), cap), :]
                same = jnp.concatenate([same] * TOGETHER, axis=0)
                row_at = lax.broadcasted_iota(jnp.int32, (cap, seen_keys), 0) + place * cap
                seen = lax.broadcasted_iota(jnp.int32, (cap, seen_keys), 1) <= row_at
                for begin in range(0, heads, TOGETHER):
                    tiles = [block_q[:, head * LANES : (head + 1) * LANES] for head in range(begin, begin + TOGETHER)]
                    tile_q = jnp.concatenate([jnp.concatenate(tiles, axis=0), same], axis=1)
                    raw = scores(tile_q, keys(ok_ref[:seen_keys], od_ref[:seen_keys]))
                    raw = jnp.where(seen[None], raw.reshape(TOGETHER, cap, seen_keys), NEVER)
                    tile_qs.append(tile_q)
                    raws.append([raw.reshape(TOGETHER * cap, seen_keys)])
            tile_vs = [ov_ref[:seen_keys]]
            if with_past:
                for several, tile_q in zip(raws, tile_qs):
                    several.append(scores(tile_q, keys(pk_ref[0], pd_ref[0])))
                tile_vs.append(pv_ref[0])
            peaks = [functools.reduce(jnp.maximum, [top(raw) for raw in several]) for several in raws]
            mixes = [
                sum(mix(raw, peak, values(tile_v)) for raw, tile_v in zip(several, tile_vs))
                for several, peak in zip(raws, peaks)
            ]
            if count > 1:

                def step(earlier, state):
                    result = []
                    for (peak, mixed), tile_q in zip(state, tile_qs):
                        raw = scores(tile_q, keys(pk_ref[earlier], pd_ref[earlier]))
                        higher = jnp.maximum(peak, top(raw))
                        decay = jnp.exp2((peak - higher) * factor)
                        result.append((higher, mixed * decay + mix(raw, higher, values(pv_ref[earlier]))))
                    return result

                low = functools.reduce(jnp.minimum, [low_of(place) for place in places])
                least = jnp.maximum(low + meta_ref[0] * rows, 0) // rows
                mixes = [mixed for _, mixed in lax.fori_loop(least, meta_ref[0], step, list(zip(peaks, mixes)))]
            groups = heads // TOGETHER
            for at, mixed in enumerate(mixes):
                result = (mixed[:, :LANES] / mixed[:, LANES:]).astype(jnp.bfloat16)
                for head in range(TOGETHER):
                    column = (at % groups * TOGETHER + head) * LANES
                    result_ref[indices[at // groups], :, column : column + LANES] = result[head * cap : (head + 1) * cap]

        def body(pair, carry):
            indices = [list_ref[2 * pair], list_ref[2 * pair + 1]]
            places = [place_of(index) for index in indices]
            low = jnp.minimum(*[low_of(place) for place in places])
            short = jnp.maximum(*places) < blocks // 2
            for seen_keys, here in ((half, short), (rows, jnp.logical_not(short))):
                if count > 1:
                    pl.when(here)(functools.partial(some_blocks, indices, places, seen_keys, False))
                else:
                    pl.when(here & (low >= 0))(functools.partial(some_blocks, indices, places, seen_keys, False))
                    pl.when(here & (low < 0))(functools.partial(some_blocks, indices, places, seen_keys, True))
            result_copy(indices[0]).start()
            pl.when(indices[0] != indices[1])(result_copy(indices[1]).start)
            return carry

        held = jnp.int32(0)
        for index in range(parcels):
            list_ref[held] = index
            held += jnp.where(place_of(index) < blocks, 1, 0)
        list_ref[held] = list_ref[jnp.maximum(held - 1, 0)]

        for index in range(parcels):

            @pl.when(place_of(index) < blocks)
            def _():
                stage_ref[index] = array_refs[0][index] if index < slots else array_refs[index - slots + (slots > 0)][...]

        lax.fori_loop(0, (held + 1) // 2, body, 0)
        for index in range(parcels):
            pl.when(place_of(index) < blocks)(result_copy(index).wait)

    operands = [meta, *own, *past, *arrays]
    specs = [SMEM] + [VMEM] * (len(operands) - 1)
    aliases = {}
    if out is not None:
        aliases = {len(operands): 0}
        operands.append(out)
        specs.append(ANY)
    area = max(1, parcels // 2) * heads * cap * (count + 1) * rows
    return pl.pallas_call(
        kernel,
        out_shape=jax.ShapeDtypeStruct((rows, width), jnp.bfloat16),
        in_specs=specs,
        out_specs=ANY,
        input_output_aliases=aliases,
        scratch_shapes=[
            pltpu.VMEM((parcels, cap, width), jnp.bfloat16),
            pltpu.VMEM((parcels, cap, width), jnp.bfloat16),
            pltpu.SMEM((parcels + 1,), jnp.int32),
            pltpu.SemaphoreType.DMA((parcels,)),
        ],
        compiler_params=params(28),
        cost_estimate=pl.CostEstimate(
            flops=8 * area * LANES, bytes_accessed=4 * parcels * cap * width, transcendentals=area
        ),
        name="attend",
    )(*operands)


def digits(begin):
    lane = jnp.arange(LANES, dtype=jnp.int32)
    digit = jnp.where(lane < DIGIT, begin[..., None] // DIGIT, begin[..., None] % DIGIT)
    hit = digit == lane % DIGIT
    return jnp.where(hit, 1.0, 0.0).astype(jnp.bfloat16), jnp.where(hit, 0.0, -APART).astype(jnp.bfloat16)


def local(queries, keys_values, routing, documents):
    rows, width = queries.shape
    owners = lax.axis_size("dp")
    columns = lax.axis_size("ctx")
    kv_heads, pair, head_dim = keys_values.shape[1:]
    assert kv_heads == 1 and pair == 2 and head_dim == LANES
    cap = 2 * rows // owners
    blocks = rows // cap
    seq_len = rows * columns
    assert seq_len <= DIGIT * DIGIT
    half = owners // 2
    assert owners & (owners - 1) == 0
    column = lax.axis_index("ctx")
    me = lax.axis_index("dp")

    routing = routing.T
    send_kv = pack_kv(routing, documents.reshape(-1, LANES), keys_values.reshape(2 * rows, LANES), owners, seq_len)
    parcels = lax.all_to_all(send_kv, "dp", split_axis=0, concat_axis=0, tiled=True)
    near, *far = pack_q(routing, queries, send_kv, owners)
    groups = [list(range(half)), list(range(half, owners))]
    near = lax.all_to_all(near, "dp", split_axis=0, concat_axis=0, axis_index_groups=groups, tiled=True)
    label = parcels[:, :4].astype(jnp.float32).astype(jnp.int32)
    place, part = label[:, 2, 0], label[:, 3, 0]
    begin = (label[:, 0] * DIGIT + label[:, 1]).reshape(owners, LANES // cap, cap)
    slots = jnp.arange(blocks, dtype=jnp.int32)
    every = jnp.arange(owners, dtype=jnp.int32)
    chosen = place[None, :] == slots[:, None]
    source = jnp.sum(jnp.where(chosen, every[None, :], 0), axis=1)
    senders = jnp.concatenate([me // half * half + every[:half], me ^ every[half:]])
    places = jnp.sum(jnp.where(senders[:, None] == every[None, :], place[None, :], 0), axis=1)
    wanted = chosen[:, :, None] & (part[None, :, None] == jnp.arange(LANES // cap, dtype=jnp.int32))
    doc = jnp.sum(jnp.where(wanted[..., None], begin[None], 0), axis=(1, 2)).reshape(rows)

    split = jnp.concatenate([doc // DIGIT, doc % DIGIT]).astype(jnp.float32).astype(jnp.bfloat16).reshape(-1, LANES)
    split = jnp.pad(split, ((0, -split.shape[0] % LABEL_ROWS), (0, 0)))
    own_kv = place_kv(source, parcels, split, rows, cap)
    past_kv = lax.ppermute(own_kv, "ctx", [(0, 1)])[None] if columns == 2 else lax.all_gather(own_kv, "ctx")
    same, apart = digits(doc)
    own = (same, own_kv[: 2 * rows].reshape(rows, 2, LANES)[:, 0], apart, own_kv[: 2 * rows].reshape(rows, 2, LANES)[:, 1])
    past_doc = past_kv[:, 2 * rows :][:, : 2 * rows // LANES].reshape(-1, 2, rows).astype(jnp.float32).astype(jnp.int32)
    past_apart = digits(past_doc[:, 0] * DIGIT + past_doc[:, 1])[1]
    past_rows = past_kv[:, : 2 * rows].reshape(-1, rows, 2, LANES)
    past = (past_rows[:, :, 0], past_apart, past_rows[:, :, 1])

    lows = jnp.min(doc.reshape(blocks, cap), axis=1) - column * rows
    meta = jnp.concatenate([column[None], places, lows])
    sent, far = far, []
    for index, parcel in enumerate(sent):
        if index >= 4:
            ties = (past_kv,) if index >= half - 2 else (far[index - 4], own_kv)
            parcel = lax.optimization_barrier((parcel, *ties))[0]
        far.append(lax.ppermute(parcel, "dp", [(owner, owner ^ (half + index)) for owner in range(owners)]))
    out = attend(meta, half, None, far[: half - 4], own, past, None)
    out = attend(meta, half + half - 4, None, far[half - 4 : half - 2], own, past, out)
    out = attend(meta, 0, near, [], own, past, out)
    return attend(meta, half + half - 2, None, far[half - 2 :], own, past, out)


def solution(mesh):
    placed = (
        P(("dp", "ctx"), None),
        P(("dp", "ctx"), None, None, None),
        P(("dp", "ctx"), None),
        P(("dp", "ctx")),
    )
    return jax.shard_map(
        local, mesh=mesh, in_specs=placed, out_specs=P(("dp", "ctx"), None), check_vma=False
    )
```
